256 devices in a mesh: dp: 16 (over x, y_hi, core), tensor: 16 (over y_lo, z).
Axes of the slice: x: 4, y: 4 (y_hi: 2, y_lo: 2; y = y_hi * 2 + y_lo), z: 8, core: 2. Of those that a mesh axis runs over, the one named last changes fastest.
Arguments:
- inputs: bfloat16 [32768, 5120], P(('dp', 'tensor')), may hold values from -6 to 6
- latent: bfloat16 [32768, 512], P(('dp', 'tensor')), may hold values from -180 to 180
- gain: float32 [512], replicated, may hold values from 0.25 to 1.75
- w_latent: bfloat16 [5120, 512], P('tensor'), may hold values from -0.078125 to 0.078125
- w_rope: bfloat16 [5120, 64], P('tensor'), may hold values from -0.078125 to 0.078125
- w_up: bfloat16 [512, 32768], P('dp', 'tensor'), may hold values from -0.25 to 0.25
- grad_kv: bfloat16 [32768, 32768], P('dp', 'tensor'), may hold values from -6 to 6
- grad_rope: bfloat16 [32768, 64], P(('dp', 'tensor')), may hold values from -6 to 6
Outputs:
- grad_x: bfloat16 [32768, 5120], P(('dp', 'tensor'))
- grad_w_up: bfloat16 [512, 32768], P('dp', 'tensor')
- grad_w_latent: bfloat16 [5120, 512], P('tensor', 'dp')
- grad_w_rope: bfloat16 [5120, 64], P('tensor', 'dp')
- grad_gain: float32 [512], replicated
The draws below stay inside these ranges and needn't reach their ends.
All inputs are finite; a program needn't handle non-finite values.
Results may differ from the reference program's by a relative error of at most 0.019.
Values may be sent and summed in bfloat16 or wider, within the bound.
A program may use at most 128 MiB of HBM per device.

```python
import math
import jax
import jax.numpy as jnp
from jax import lax

D = 5120
LAT = 512
ROPE = 64
HEADS = 128
HDIM = 128
VDIM = 128
TOKENS = 32768


def draw_latent(key, part):
    key = jax.random.fold_in(key, 7)
    key_base, key_rows, key_cols = jax.random.split(key, 3)
    row_scale = jnp.exp(jax.random.uniform(key_rows, (TOKENS, 1), minval=0.0, maxval=math.log(10.0)))
    col_scale = jnp.exp(jax.random.uniform(key_cols, (1, LAT), minval=0.0, maxval=math.log(10.0)))
    base_values = jax.random.normal(key_base, (TOKENS, LAT))
    base_values = jnp.clip(base_values, -6.0, 6.0)
    return (base_values * row_scale * col_scale * 0.3).astype(jnp.bfloat16)


def block_scale(own_key, shape, cuts, least, largest):
    loudness = 1.0
    for axis_at, shards_of in cuts:
        draws = jax.random.uniform(jax.random.fold_in(jax.random.fold_in(own_key, 6), axis_at), (shards_of,), jnp.float32, least / len(cuts), largest / len(cuts))
        loudness = loudness * jnp.repeat(jnp.exp(draws), shape[axis_at] // shards_of).reshape((-1,) + (1,) * (len(shape) - 1 - axis_at))
    return loudness


def centred(key, dims, width, limit, cuts=(), held_as=jnp.bfloat16):
    result = jax.random.normal(key, dims, jnp.float32) * width
    if len(cuts) > 0:
        result = block_scale(key, dims, cuts, -0.22, 0.18) * result
    return jnp.clip(result, min=-limit, max=limit).astype(held_as)


def setup_inputs(seed: int = 0) -> dict:
    key_of = jax.random.split(jax.random.key(seed), 9)
    inputs = centred(key_of[0], (TOKENS, D), 1.0, 6.0, ((0, 256),))
    latent = draw_latent(jax.random.fold_in(key_of[8], 71), 0)
    gain = jnp.clip(1.0 + 0.15 * jax.random.normal(key_of[2], (LAT,), jnp.float32), 0.25, 1.75)
    w_latent = centred(key_of[3], (D, LAT), D ** -0.5, 0.078125, ((0, 16),))
    w_rope = centred(key_of[4], (D, ROPE), D ** -0.5, 0.078125, ((0, 16),))
    w_up = centred(key_of[5], (LAT, HEADS * (HDIM + VDIM)), LAT ** -0.5, 0.25, ((0, 16), (1, 16)))
    grad_kv = centred(key_of[6], (TOKENS, HEADS * (HDIM + VDIM)), 1.0, 6.0, ((0, 16), (1, 16)))
    grad_rope = centred(key_of[7], (TOKENS, ROPE), 1.0, 6.0, ((0, 256),))
    return {"inputs": inputs, "latent": latent, "gain": gain, "w_latent": w_latent, "w_rope": w_rope, "w_up": w_up, "grad_kv": grad_kv, "grad_rope": grad_rope}


epsilon = 1e-06

def reference(inputs, latent, gain, w_latent, w_rope, w_up, grad_kv, grad_rope):
    latent_f = latent.astype(jnp.float32)
    inverse = lax.rsqrt(lax.optimization_barrier(jnp.mean(latent_f * latent_f, axis=-1, keepdims=True)) + epsilon)
    normed = (latent_f * inverse * gain).astype(jnp.bfloat16)
    grad_w_up = jnp.dot(normed.T, grad_kv, preferred_element_type=jnp.float32).astype(jnp.bfloat16)
    grad_norm = jnp.dot(grad_kv, w_up.T, preferred_element_type=jnp.float32)
    grad_gain = lax.optimization_barrier(jnp.sum(grad_norm * latent_f * inverse, axis=0))
    scaled = grad_norm * gain
    grad_pre = inverse * scaled - latent_f * inverse ** 3 * lax.optimization_barrier(jnp.mean(scaled * latent_f, axis=-1, keepdims=True))
    grad_pre = grad_pre.astype(jnp.bfloat16)
    grad_x = jnp.dot(grad_pre, w_latent.T, preferred_element_type=jnp.float32) + jnp.dot(grad_rope, w_rope.T, preferred_element_type=jnp.float32)
    grad_w_latent = jnp.dot(inputs.T, grad_pre, preferred_element_type=jnp.float32)
    grad_w_rope = jnp.dot(inputs.T, grad_rope, preferred_element_type=jnp.float32)
    return (grad_x.astype(jnp.bfloat16), grad_w_up, grad_w_latent.astype(jnp.bfloat16), grad_w_rope.astype(jnp.bfloat16), grad_gain)
```

```python
import jax
import jax.numpy as jnp
from jax import lax
from jax.experimental import pallas as pl
from jax.experimental.pallas import tpu as pltpu
from jax.sharding import PartitionSpec as P

MESH = pl.DeviceIdType.MESH
epsilon = 1e-06
f32 = jnp.float32
bf16 = jnp.bfloat16

SENDS = 200
RECVS = 200


def nt(a, b):
    return lax.dot_general(a, b, (((1,), (1,)), ((), ())), preferred_element_type=f32)


def nn(a, b):
    return lax.dot_general(a, b, (((1,), (0,)), ((), ())), preferred_element_type=f32)


class Place:
    def __init__(self):
        dp = lax.axis_index("dp")
        t = lax.axis_index("tensor")
        self.x = dp // 4
        self.yh = (dp // 2) % 2
        self.c = dp % 2
        self.yl = t // 8
        self.z = t % 8
        self.dp = dp
        self.t = t

    def dev(self, x=None, yh=None, c=None, yl=None, z=None):
        x = self.x if x is None else x
        yh = self.yh if yh is None else yh
        c = self.c if c is None else c
        yl = self.yl if yl is None else yl
        z = self.z if z is None else z
        return (x * 4 + yh * 2 + c, yl * 8 + z)

    def at_x(self, o):
        return (self.x + o) % 4

    def at_z(self, o):
        return (self.z + o + 8) % 8

    def at_y(self, o):
        y = (self.yh * 2 + self.yl + o) % 4
        return y // 2, y % 2

    def dev_x(self, o):
        return self.dev(x=self.at_x(o))

    def dev_z(self, o):
        return self.dev(z=self.at_z(o))

    def dev_y(self, o):
        yh, yl = self.at_y(o)
        return self.dev(yh=yh, yl=yl)


class Mail:
    def __init__(self, send_sem, recv_sem):
        self.send_sem = send_sem
        self.recv_sem = recv_sem
        self.sent = 0
        self.slots = 0
        self.open = []

    def slot(self, n=1):
        at = self.slots
        self.slots += n
        assert self.slots <= RECVS
        return at

    def send(self, src, dst, slot, device):
        at = self.sent
        self.sent += 1
        assert self.sent <= SENDS
        copy = pltpu.make_async_remote_copy(
            src_ref=src,
            dst_ref=dst,
            send_sem=self.send_sem.at[at],
            recv_sem=self.recv_sem.at[slot],
            device_id=device,
            device_id_type=MESH,
        )
        copy.start()
        self.open.append(copy)

    def wait(self, dst, slot, device):
        pltpu.make_async_remote_copy(
            src_ref=dst,
            dst_ref=dst,
            send_sem=self.send_sem.at[0],
            recv_sem=self.recv_sem.at[slot],
            device_id=device,
            device_id_type=MESH,
        ).wait_recv()

    def finish(self):
        for copy in self.open:
            copy.wait_send()


class Gather:
    def __init__(self, place, mail, block):
        self.p, self.m, self.block = place, mail, block
        self.plus = [mail.slot() for _ in range(4)]
        self.minus = [mail.slot() for _ in range(4)]

    def arrive(self, s):
        p, m = self.p, self.m
        part = (None, None) if s < 4 else (0, 1)
        m.wait(self.block(p.at_z(-s), part[0]), self.plus[s - 1], p.dev_z(1))
        m.wait(self.block(p.at_z(s), part[1]), self.minus[s - 1], p.dev_z(-1))

    def forward(self, s):
        p, m = self.p, self.m
        part = (None, None) if s < 3 else (0, 1)
        low, high = self.block(p.at_z(-s), part[0]), self.block(p.at_z(s), part[1])
        m.send(low, low, self.plus[s], p.dev_z(1))
        m.send(high, high, self.minus[s], p.dev_z(-1))


class Scatter:
    def __init__(self, place, mail, part, rows, out, plus, minus):
        self.p, self.m, self.part, self.rows = place, mail, part, rows
        self.out, self.rp, self.rm = out, plus, minus
        self.plus = [mail.slot() for _ in range(4)]
        self.minus = [mail.slot() for _ in range(4)]

    def step(self, s):
        p, m, rows = self.p, self.m, self.rows
        half = rows // 2
        if s == 0:
            self.out[0] = self.part(0, 0, rows).astype(bf16)
            m.send(self.out.at[0, pl.ds(0, half)], self.rp.at[0, pl.ds(0, half)], self.plus[0], p.dev_z(1))
            m.send(self.out.at[0, pl.ds(half, half)], self.rm.at[0, pl.ds(half, half)], self.minus[0], p.dev_z(-1))
            return
        for way, got, slots, k in ((1, self.rp, self.plus, 2 * s - 1), (-1, self.rm, self.minus, 2 * s)):
            if s == 1:
                lo = 0 if way == 1 else half
                other = half - lo
                m.wait(got.at[0, pl.ds(lo, half)], slots[0], p.dev_z(way))
                self.out[k, lo : lo + half] = (
                    self.part(k, lo, lo + half) + got[0, lo : lo + half].astype(f32)
                ).astype(bf16)
                self.out[k, other : other + half] = self.part(k, other, other + half).astype(bf16)
            else:
                m.wait(got.at[s - 1], slots[s - 1], p.dev_z(way))
                self.out[k] = (self.part(k, 0, rows) + got[s - 1].astype(f32)).astype(bf16)
            m.send(self.out.at[k], got.at[s], slots[s], p.dev_z(way))

    def last(self):
        p, m = self.p, self.m
        m.wait(self.rp.at[3], self.plus[3], p.dev_z(1))
        m.wait(self.rm.at[3], self.minus[3], p.dev_z(-1))
        return self.part(7, 0, self.rows) + self.rp[3].astype(f32) + self.rm[3].astype(f32)


def kernel(
    inputs, latent, gain, w_latent, w_rope, w_up, kv_hbm, grad_rope,
    gx, gup, glat, grope, ggain,
    kv, up, nrm, part, ga_out, ga_p, ga_m, gy_out, gy_in, gb_out, gb_p, gb_m, gay_out, gay_in,
    wx, wc, intr, ins, pre, pres, gxs,
    gw, r1, r2, a1, a2, s3, s3p, s3m, a3x, r3x, ry, rx, a12, r12, a3y, r3y, fin, rfin,
    gus, gusi, gu, gui, guy, guyi, guz, gn, rgz, rgy, rgx, rgc, gns,
    kv_sem, send_sem, recv_sem,
):
    p = Place()
    m = Mail(send_sem, recv_sem)
    x, yh, c, yl, z = p.x, p.yh, p.c, p.yl, p.z
    sib = p.dev(c=1 - c)
    ylo = p.dev(yl=1 - yl)
    ylo_other = p.dev(yl=1 - yl, c=1 - c)
    yhi = p.dev(yh=1 - yh)
    yhi_other = p.dev(yh=1 - yh, c=1 - c)

    load_kv = pltpu.make_async_copy(kv_hbm, kv, kv_sem.at[0])
    load_kv.start()

    friends = [sib, ylo_other, yhi_other]
    friends += [p.dev_y(o) for o in (1, 2, 3)] + [p.dev_x(o) for o in (1, 2, 3)]
    friends += [p.dev_z(o) for o in range(1, 8)]
    barrier = pltpu.get_barrier_semaphore()
    for friend in friends:
        pl.semaphore_signal(barrier, inc=1, device_id=friend, device_id_type=MESH)
    pl.semaphore_wait(barrier, len(friends))

    ux = [m.slot() for _ in range(6)]
    uyh = m.slot()
    usib = [m.slot() for _ in range(8)]

    def ublock(xx, hh, cc):
        return up.at[xx * 4 + hh * 2 + cc]

    mine = ublock(x, yh, c)
    m.send(w_up, mine, uyh, yhi)
    for o in (1, 3, 2):
        m.send(w_up, mine, ux[o - 1], p.dev_x(o))
    m.send(w_up, mine, usib[0], sib)
    up[p.dp] = w_up[...]

    lat = latent[...].astype(f32)
    inverse = lax.rsqrt(jnp.mean(lat * lat, axis=-1, keepdims=True) + epsilon)
    normed = lat * inverse * gain[...]
    nrm[yl, z] = normed.T.astype(bf16)

    def nblock_a(zz, half):
        if half is None:
            return nrm.at[:, zz, pl.ds(0, 256)]
        return nrm.at[half, zz, pl.ds(0, 256)]

    def nblock_b(zz, half):
        if half is None:
            return nrm.at[yl, zz, pl.ds(256, 256)]
        return nrm.at[yl, zz, pl.ds(256 + 128 * half, 128)]

    na = Gather(p, m, nblock_a)
    nb = Gather(p, m, nblock_b)
    nay = m.slot()
    nby = [m.slot() for _ in range(8)]

    def nb_over(zz, slot):
        block = nrm.at[yl, zz, pl.ds(256, 256)]
        m.send(block, block, nby[slot], ylo)

    def nb_arrive(zz, slot):
        m.wait(nrm.at[1 - yl, zz, pl.ds(256, 256)], nby[slot], ylo)

    first = nrm.at[yl, z, pl.ds(0, 256)]
    m.send(first, first, nay, ylo)
    nb.forward(0)
    nb_over(z, 0)

    wx[:, 0:512] = w_latent[...]
    wx[:, 512:576] = w_rope[...]
    wx[:, 576:640] = jnp.zeros((320, 64), bf16)
    quarter = pl.ds(pl.multiple_of(80 * x, 16), 80)
    wy = m.slot()

    def wblock(zz, half):
        if half is None:
            return wc.at[zz, quarter]
        return wc.at[zz, pl.ds(pl.multiple_of(80 * x + 48 * half, 16), 48 - 16 * half)]

    wg = Gather(p, m, wblock)
    local = pltpu.make_async_copy(wx.at[quarter], wblock(z, None), kv_sem.at[1])

    @pl.when(c == yl)
    def _():
        local.start()
        local.wait()

    across = pltpu.make_async_remote_copy(
        src_ref=wx.at[quarter],
        dst_ref=wblock(z, None),
        send_sem=send_sem.at[SENDS],
        recv_sem=recv_sem.at[wy],
        device_id=ylo_other,
        device_id_type=MESH,
    )

    @pl.when(c != yl)
    def _():
        across.start()

    def turn(i, carry):
        piece = inputs[:, pl.ds(pl.multiple_of(i * 640, 128), 640)].T
        for j in range(2):
            for h in range(2):
                lo = j * 320 + h * 160
                intr[h, 2 * i + j] = piece[lo : lo + 160]
        return carry

    m.wait(nrm.at[1 - yl, z, pl.ds(0, 256)], nay, ylo)
    na.forward(0)
    m.wait(ublock(x, 1 - yh, c), uyh, yhi)
    theirs = ublock(x, 1 - yh, c)
    for o in (1, 3, 2):
        m.send(theirs, theirs, ux[2 + o], p.dev_x(o))
    m.send(theirs, theirs, usib[1], sib)

    lax.fori_loop(0, 8, turn, 0)
    ins_slot = m.slot()
    m.send(intr.at[1 - c], ins, ins_slot, sib)
    pre[:, 512:576] = grad_rope[...]
    pre[:, 576:640] = jnp.zeros((128, 64), bf16)

    @pl.when(c != yl)
    def _():
        across.wait_send()
        across.wait_recv()

    nb.arrive(1)
    nb.forward(1)
    nb_over(p.at_z(-1), 1)
    nb_over(p.at_z(1), 2)
    na.arrive(1)
    na.forward(1)
    wg.forward(0)
    for i, o in enumerate((1, 3, 2)):
        theirs = ublock(p.at_x(-o), yh, c)
        m.wait(theirs, ux[o - 1], p.dev_x(o))
        m.send(theirs, theirs, usib[2 + i], sib)
    nb.arrive(2)
    nb.forward(2)
    nb_over(p.at_z(-2), 3)
    nb_over(p.at_z(2), 4)
    na.arrive(2)
    na.forward(2)
    wg.arrive(1)
    wg.forward(1)
    for i, o in enumerate((1, 3, 2)):
        theirs = ublock(p.at_x(-o), 1 - yh, c)
        m.wait(theirs, ux[2 + o], p.dev_x(o))
        m.send(theirs, theirs, usib[5 + i], sib)
    load_kv.wait()
    m.wait(ublock(x, yh, 1 - c), usib[0], sib)
    m.wait(ublock(x, 1 - yh, 1 - c), usib[1], sib)
    for i, o in enumerate((1, 3, 2)):
        m.wait(ublock(p.at_x(-o), yh, 1 - c), usib[2 + i], sib)
        m.wait(ublock(p.at_x(-o), 1 - yh, 1 - c), usib[5 + i], sib)

    def compute(k):
        away = 4 - (k + 1) // 2
        zd = (z + 8 + (2 * (k % 2) - 1) * away) % 8
        rows = kv[:, zd].reshape(256, 2048)
        got = nt(rows, up[...].reshape(512, 2048))
        part[k] = got.reshape(2, 128, 512)
        gy_out[k] = part[k, 1 - yl, :, 256:512].astype(bf16)

    ay = Scatter(p, m, lambda k, lo, hi: part[k, :, :, 0:256].reshape(256, 256)[lo:hi], 256, ga_out, ga_p, ga_m)

    def part_b(k, lo, hi):
        return part[k, yl, lo:hi, 256:512] + gy_in[k, lo:hi].astype(f32)

    by = Scatter(p, m, part_b, 128, gb_out, gb_p, gb_m)
    gys = [m.slot() for _ in range(8)]

    def over(k):
        m.send(gy_out.at[k], gy_in.at[k], gys[k], ylo)

    def over_in(k):
        m.wait(gy_in.at[k], gys[k], ylo)

    compute(0)
    ay.step(0)
    over(0)

    def more(k, carry):
        compute(k)
        return carry

    lax.fori_loop(1, 3, more, 0)
    over(1)
    over(2)
    over_in(0)
    by.step(0)
    lax.fori_loop(3, 8, more, 0)
    for k in range(3, 8):
        over(k)
    nb.arrive(3)
    nb.forward(3)
    nb_over(p.at_z(-3), 5)
    nb_over(p.at_z(3), 6)
    na.arrive(3)
    na.forward(3)
    ay.step(1)
    over_in(1)
    over_in(2)
    by.step(1)
    nb.arrive(4)
    nb_over(p.at_z(4), 7)
    na.arrive(4)
    wg.arrive(2)
    wg.forward(2)
    ay.step(2)
    over_in(3)
    over_in(4)
    by.step(2)
    for i, zz in enumerate((z, p.at_z(-1), p.at_z(1), p.at_z(-2), p.at_z(2), p.at_z(-3), p.at_z(3), p.at_z(4))):
        nb_arrive(zz, i)

    def up_tile(j):
        left = jnp.concatenate([nrm[i // 8, i % 8] for i in range(16)], axis=1)
        right = kv[:, :, :, pl.ds(pl.multiple_of(j * 256, 128), 256)].reshape(2048, 256)
        return nn(left, right)

    def theirs_tile(i, carry):
        gus[i] = up_tile(4 * (1 - c) + i).astype(bf16)
        return carry

    lax.fori_loop(0, 4, theirs_tile, 0)
    gus_slot = m.slot()
    m.send(gus, gusi, gus_slot, sib)
    wg.arrive(3)
    wg.forward(3)
    ay.step(3)
    over_in(5)
    over_in(6)
    by.step(3)
    m.wait(gusi, gus_slot, sib)

    def mine_tile(i, carry):
        gu[:, i] = (up_tile(4 * c + i) + gusi[i].astype(f32)).astype(bf16).reshape(4, 128, 256)
        return carry

    lax.fori_loop(0, 4, mine_tile, 0)
    gux = [m.slot() for _ in range(3)]
    for o in (1, 3, 2):
        m.send(gu.at[p.at_x(o)], gui.at[o - 1], gux[o - 1], p.dev_x(o))

    over_in(7)
    half_b = by.last()
    half_a = ay.last().reshape(2, 128, 256)
    gay_out[...] = half_a.astype(bf16)
    gay_slot = m.slot()
    m.send(gay_out.at[1 - yl], gay_in, gay_slot, ylo)

    wg.arrive(4)
    wxs = [m.slot() for _ in range(4)]

    def wquarter(xx, lo, n):
        return wc.at[pl.ds(lo, n), pl.ds(pl.multiple_of(80 * xx, 16), 80)]

    m.send(wquarter(x, 0, 8), wquarter(x, 0, 8), wxs[0], p.dev_x(1))
    m.send(wquarter(x, 0, 8), wquarter(x, 0, 8), wxs[1], p.dev_x(-1 + 4))

    m.wait(gay_in, gay_slot, ylo)
    part[0, 0, :, 0:256] = half_a[0]
    part[0, 1, :, 0:256] = half_a[1]
    own_a = part[0, yl, :, 0:256] + gay_in[...].astype(f32)
    grad_norm = jnp.concatenate([own_a, half_b], axis=1)
    lat = latent[...].astype(f32)
    inverse = lax.rsqrt(jnp.mean(lat * lat, axis=-1, keepdims=True) + epsilon)
    scaled = grad_norm * gain[...]
    inner = jnp.mean(scaled * lat, axis=-1, keepdims=True)
    pre[:, 0:512] = (inverse * scaled - lat * (inverse * inverse * inverse) * inner).astype(bf16)
    pre_slot = m.slot()
    m.send(pre, pres, pre_slot, sib)
    gsum = jnp.sum(grad_norm * lat * inverse, axis=0, keepdims=True)
    gn[...] = jnp.zeros((8, 128), f32)
    for q in range(4):
        gn[q : q + 1, :] = gsum[:, 128 * q : 128 * q + 128]
    rgz_slots = [m.slot() for _ in range(7)]
    for o in range(1, 8):
        m.send(gn, rgz.at[o - 1], rgz_slots[o - 1], p.dev_z(o))

    m.wait(ins, ins_slot, sib)
    m.wait(pres, pre_slot, sib)
    both = jnp.concatenate([pre[...], pres[...]], axis=0)

    def gw_tile(i, carry):
        at = pl.ds(4 * i, 4)
        left = jnp.concatenate(
            [intr[c, at].reshape(640, 128), ins[at].reshape(640, 128)], axis=1
        )
        got = nn(left, both[:, 0:512]).astype(bf16)
        for q in range(4):
            gw[q, at] = got[:, 128 * q : 128 * q + 128].reshape(4, 160, 128)
        return carry

    lax.fori_loop(0, 4, gw_tile, 0)
    r1_slots = [m.slot() for _ in range(3)]
    r2_slots = [m.slot() for _ in range(3)]
    for o in (2, 1, 3):
        m.send(gw.at[p.at_x(o), :, pl.ds(0, 64)], r1.at[o - 1], r1_slots[o - 1], p.dev_x(o))
        hh, ll = p.at_y(o)
        m.send(
            gw.at[:, pl.ds(8 * ll, 8), pl.ds(pl.multiple_of(64 + 32 * hh, 16), 32)],
            r2.at[o - 1], r2_slots[o - 1], p.dev_y(o),
        )

    zero = jnp.zeros((256, 64), bf16)
    rope = both[:, 512:576]
    rope_lo = jnp.concatenate([rope, zero], axis=1)
    rope_hi = jnp.concatenate([zero, rope], axis=1)

    def z3(k):
        away = 4 - (k + 1) // 2
        sign = 1 if k % 2 else -1
        return (z + 8 + sign * away) % 8

    def part3(k, lo, hi):
        zd = z3(k)
        low = jnp.concatenate([intr[c, zd], ins[zd]], axis=1)
        high = jnp.concatenate([intr[c, 8 + zd], ins[8 + zd]], axis=1)
        turned = nn(low, rope_lo) + nn(high, rope_hi)
        pieces = []
        for q in range(4):
            for ll in range(2):
                pieces.append(gw[q, 8 * ll + zd, 128:160, :].astype(f32))
        return jnp.concatenate(pieces + [turned], axis=0)[lo:hi]

    zs = Scatter(p, m, part3, 416, s3, s3p, s3m)
    for s in range(4):
        zs.step(s)
    sum3 = zs.last()
    for q in range(4):
        a3x[q, 0:64] = sum3[64 * q : 64 * q + 64].astype(bf16)
        a3x[q, 64:224] = sum3[256:416].astype(bf16)
    r3x_slots = [m.slot() for _ in range(3)]
    for o in (2, 1, 3):
        m.send(a3x.at[p.at_x(o)], r3x.at[o - 1], r3x_slots[o - 1], p.dev_x(o))

    for o in range(1, 8):
        m.wait(rgz.at[o - 1], rgz_slots[o - 1], p.dev_z(o))
    gns[0] = gn[...] + jnp.sum(rgz[...], axis=0)
    rgy_slots = [m.slot() for _ in range(3)]
    for o in (1, 2, 3):
        m.send(gns.at[0], rgy.at[o - 1], rgy_slots[o - 1], p.dev_y(o))

    for o in (1, 3, 2):
        m.wait(r1.at[o - 1], r1_slots[o - 1], p.dev_x(o))
    for h in range(2):
        rows = pl.ds(32 * h, 32)
        sum1 = gw[x, :, rows].astype(f32)
        for o in range(3):
            sum1 = sum1 + r1[o, :, rows].astype(f32)
        a1[h] = sum1.astype(bf16)
    ry_slots = [m.slot() for _ in range(3)]
    for o in (2, 1, 3):
        hh, ll = p.at_y(o)
        m.send(a1.at[hh, pl.ds(8 * ll, 8)], ry.at[o - 1], ry_slots[o - 1], p.dev_y(o))
    for o in (1, 3, 2):
        m.wait(r2.at[o - 1], r2_slots[o - 1], p.dev_y(o))
    for q in range(4):
        sum2 = gw[q, pl.ds(8 * yl, 8), pl.ds(pl.multiple_of(64 + 32 * yh, 16), 32)].astype(f32)
        for o in range(3):
            sum2 = sum2 + r2[o, q].astype(f32)
        a2[q] = sum2.astype(bf16)
    rx_slots = [m.slot() for _ in range(3)]
    for o in (2, 1, 3):
        m.send(a2.at[p.at_x(o)], rx.at[o - 1], rx_slots[o - 1], p.dev_x(o))

    for o in (1, 2, 3):
        m.wait(rgy.at[o - 1], rgy_slots[o - 1], p.dev_y(o))
    gns[1] = gns[0] + rgy[0] + rgy[1] + rgy[2]
    rgx_slots = [m.slot() for _ in range(3)]
    for o in (1, 2, 3):
        m.send(gns.at[1], rgx.at[o - 1], rgx_slots[o - 1], p.dev_x(o))

    for o in (1, 3, 2):
        m.wait(r3x.at[o - 1], r3x_slots[o - 1], p.dev_x(o))
    sum3 = a3x[x].astype(f32) + r3x[0].astype(f32) + r3x[1].astype(f32) + r3x[2].astype(f32)
    for ll in range(2):
        for hh in range(2):
            lo = 32 * ll + 16 * hh
            a3y[2 * hh + ll, 0:16] = sum3[lo : lo + 16].astype(bf16)
            a3y[2 * hh + ll, 16:176] = sum3[64:224].astype(bf16)
    r3y_slots = [m.slot() for _ in range(3)]
    for o in (2, 1, 3):
        hh, ll = p.at_y(o)
        m.send(a3y.at[2 * hh + ll], r3y.at[o - 1], r3y_slots[o - 1], p.dev_y(o))

    for o in (1, 3, 2):
        m.wait(ry.at[o - 1], ry_slots[o - 1], p.dev_y(o))
    sum1 = a1[yh, pl.ds(8 * yl, 8)].astype(f32)
    for o in range(3):
        sum1 = sum1 + ry[o].astype(f32)
    a12[:, 0:32] = sum1.astype(bf16)
    for o in (1, 3, 2):
        m.wait(rx.at[o - 1], rx_slots[o - 1], p.dev_x(o))
    sum2 = a2[x].astype(f32)
    for o in range(3):
        sum2 = sum2 + rx[o].astype(f32)
    a12[:, 32:64] = sum2.astype(bf16)
    r12_slots = [m.slot() for _ in range(7)]
    for o in range(1, 8):
        m.send(a12.at[p.at_z(o)], r12.at[o - 1], r12_slots[o - 1], p.dev_z(o))

    for o in (1, 3, 2):
        m.wait(gui.at[o - 1], gux[o - 1], p.dev_x(o))
    for h in range(2):
        rows = pl.ds(64 * h, 64)
        total = gu[x, :, rows].astype(f32)
        for o in range(3):
            total = total + gui[o, :, rows].astype(f32)
        guy[h] = total.astype(bf16)
    guy_slot = m.slot()
    m.send(guy.at[1 - yh], guyi, guy_slot, yhi)

    m.wait(wquarter(p.at_x(3), 0, 8), wxs[0], p.dev_x(1))
    m.wait(wquarter(p.at_x(1), 0, 8), wxs[1], p.dev_x(3))
    m.send(wquarter(p.at_x(3), 0, 4), wquarter(p.at_x(3), 0, 4), wxs[2], p.dev_x(1))
    m.send(wquarter(p.at_x(1), 4, 4), wquarter(p.at_x(1), 4, 4), wxs[3], p.dev_x(3))

    m.wait(guyi, guy_slot, yhi)
    total = guy[yh].astype(f32) + guyi[...].astype(f32)
    for h in range(2):
        guz[h] = total[:, 32 * h : 32 * h + 32].astype(bf16)
    guz_slot = m.slot()
    m.send(guz.at[1 - c], gup.at[c], guz_slot, sib)
    gup[c] = guz[c]

    for o in (1, 2, 3):
        m.wait(rgx.at[o - 1], rgx_slots[o - 1], p.dev_x(o))
    gns[2] = gns[1] + rgx[0] + rgx[1] + rgx[2]
    rgc_slot = m.slot()
    m.send(gns.at[2], rgc, rgc_slot, sib)

    for o in (1, 2, 3):
        m.wait(r3y.at[o - 1], r3y_slots[o - 1], p.dev_y(o))
    sum3 = a3y[2 * yh + yl].astype(f32) + r3y[0].astype(f32) + r3y[1].astype(f32) + r3y[2].astype(f32)
    fin[64:80] = sum3[0:16].astype(bf16)
    rfin[...] = sum3[16:176].astype(bf16)
    rfin_slot = m.slot()
    m.send(rfin, grope.at[c], rfin_slot, sib)
    grope[c] = rfin[...]
    for o in range(1, 8):
        m.wait(r12.at[o - 1], r12_slots[o - 1], p.dev_z(o))
    fin[0:64] = (a12[z].astype(f32) + jnp.sum(r12[...].astype(f32), axis=0)).astype(bf16)
    fin_slots = [m.slot() for _ in range(3)]
    for slot, friend in zip(fin_slots, (sib, yhi, yhi_other)):
        m.send(fin, glat.at[c, yh], slot, friend)
    glat[c, yh] = fin[...]

    m.wait(wquarter(p.at_x(2), 0, 4), wxs[2], p.dev_x(1))
    m.wait(wquarter(p.at_x(2), 4, 4), wxs[3], p.dev_x(3))

    def gx_tile(i, carry):
        got = nt(both, wc[pl.ds(2 * i, 2)].reshape(640, 640)).astype(bf16)
        at = pl.ds(pl.multiple_of(i * 640, 128), 640)
        gx[c, :, at] = got[0:128]
        gxs[:, at] = got[128:256]
        return carry

    lax.fori_loop(0, 4, gx_tile, 0)
    gx_slot = m.slot()
    m.send(gxs, gx.at[c], gx_slot, sib)

    m.wait(rgc, rgc_slot, sib)
    ggain[...] = gns[2] + rgc[...]
    m.wait(gup.at[1 - c], guz_slot, sib)
    m.wait(grope.at[1 - c], rfin_slot, sib)
    m.wait(glat.at[1 - c, yh], fin_slots[0], sib)
    m.wait(glat.at[c, 1 - yh], fin_slots[1], yhi)
    m.wait(glat.at[1 - c, 1 - yh], fin_slots[2], yhi_other)
    m.wait(gx.at[1 - c], gx_slot, sib)
    m.finish()


def shards(inputs, latent, gain, w_latent, w_rope, w_up, grad_kv, grad_rope):
    V = lambda *shape: pltpu.VMEM(shape, bf16)
    F = lambda *shape: pltpu.VMEM(shape, f32)
    whole = pl.BlockSpec(memory_space=pltpu.VMEM)
    scratch = dict(
        kv=V(2, 8, 128, 2048), up=V(16, 32, 2048), nrm=V(2, 8, 512, 128), part=F(8, 2, 128, 512),
        ga_out=V(8, 256, 256), ga_p=V(4, 256, 256), ga_m=V(4, 256, 256),
        gy_out=V(8, 128, 256), gy_in=V(8, 128, 256),
        gb_out=V(8, 128, 256), gb_p=V(4, 128, 256), gb_m=V(4, 128, 256),
        gay_out=V(2, 128, 256), gay_in=V(128, 256),
        wx=V(320, 640), wc=V(8, 320, 640), intr=V(2, 16, 160, 128), ins=V(16, 160, 128),
        pre=V(128, 640), pres=V(128, 640), gxs=V(128, 2560),
        gw=V(4, 16, 160, 128), r1=V(3, 16, 64, 128), r2=V(3, 4, 8, 32, 128),
        a1=V(2, 16, 32, 128), a2=V(4, 8, 32, 128),
        s3=V(8, 416, 128), s3p=V(4, 416, 128), s3m=V(4, 416, 128),
        a3x=V(4, 224, 128), r3x=V(3, 224, 128), ry=V(3, 8, 32, 128), rx=V(3, 8, 32, 128),
        a12=V(8, 64, 128), r12=V(7, 64, 128), a3y=V(4, 176, 128), r3y=V(3, 176, 128),
        fin=V(80, 128), rfin=V(160, 128),
        gus=V(4, 512, 256), gusi=V(4, 512, 256), gu=V(4, 4, 128, 256), gui=V(3, 4, 128, 256),
        guy=V(2, 4, 64, 256), guyi=V(4, 64, 256), guz=V(2, 4, 32, 256),
        gn=F(8, 128), rgz=F(7, 8, 128), rgy=F(3, 8, 128), rgx=F(3, 8, 128), rgc=F(8, 128), gns=F(3, 8, 128),
        kv_sem=pltpu.SemaphoreType.DMA((2,)),
        send_sem=pltpu.SemaphoreType.DMA((SENDS + 1,)),
        recv_sem=pltpu.SemaphoreType.DMA((RECVS,)),
    )

    def body(*refs):
        own = refs[:13]
        kernel(*own, **dict(zip(scratch, refs[13:])))

    gx, gup, glat, grope, ggain = pl.pallas_call(
        body,
        out_shape=(
            jax.ShapeDtypeStruct((2, 128, 2560), bf16),
            jax.ShapeDtypeStruct((2, 4, 32, 256), bf16),
            jax.ShapeDtypeStruct((2, 2, 80, 128), bf16),
            jax.ShapeDtypeStruct((2, 160, 128), bf16),
            jax.ShapeDtypeStruct((8, 128), f32),
        ),
        in_specs=[whole] * 6 + [pl.BlockSpec(memory_space=pl.ANY), whole],
        out_specs=(whole,) * 5,
        scratch_shapes=list(scratch.values()),
        compiler_params=pltpu.CompilerParams(
            collective_id=0, has_side_effects=True, vmem_limit_bytes=60 << 20
        ),
    )(
        inputs, latent, gain.reshape(1, 512), w_latent, w_rope, w_up,
        grad_kv.reshape(2, 8, 128, 2048), grad_rope,
    )
    dp = lax.axis_index("dp")
    t = lax.axis_index("tensor")
    grad_x = gx.transpose(1, 0, 2).reshape(128, 5120)
    grad_w_up = gup.transpose(2, 0, 1, 3).reshape(32, 2048)
    rows = jnp.concatenate(
        [
            glat[:, :, 0:32].reshape(2, 64, 128),
            glat[:, :, 32:64].reshape(2, 64, 128),
            glat[:, :, 64:80].reshape(2, 32, 128),
        ],
        axis=1,
    ).reshape(320, 128)
    grad_w_latent = lax.dynamic_slice_in_dim(rows, (dp % 4) * 32, 32, axis=1)
    grad_w_rope = lax.dynamic_slice_in_dim(grope.reshape(320, 128), (t // 8) * 64 + dp * 4, 4, axis=1)
    return grad_x, grad_w_up, grad_w_latent, grad_w_rope, ggain[0:4].reshape(512)


def solution(mesh):
    in_specs = (
        P(("dp", "tensor"), None),
        P(("dp", "tensor"), None),
        P(),
        P("tensor", None),
        P("tensor", None),
        P("dp", "tensor"),
        P("dp", "tensor"),
        P(("dp", "tensor"), None),
    )
    out_specs = (
        P(("dp", "tensor"), None),
        P("dp", "tensor"),
        P("tensor", "dp"),
        P("tensor", "dp"),
        P(),
    )
    return jax.shard_map(shards, mesh=mesh, in_specs=in_specs, out_specs=out_specs, check_vma=False)
```

```python
import jax
import jax.numpy as jnp
from jax import lax
from jax.experimental import pallas as pl
from jax.experimental.pallas import tpu as pltpu
from jax.sharding import PartitionSpec as P

MESH = pl.DeviceIdType.MESH
epsilon = 1e-06
f32 = jnp.float32
bf16 = jnp.bfloat16

SENDS = 260
RECVS = 260


def nt(a, b):
    return lax.dot_general(a, b, (((1,), (1,)), ((), ())), preferred_element_type=f32)


def nn(a, b):
    return lax.dot_general(a, b, (((1,), (0,)), ((), ())), preferred_element_type=f32)


class Place:
    def __init__(self):
        dp = lax.axis_index("dp")
        t = lax.axis_index("tensor")
        self.x = dp // 4
        self.yh = (dp // 2) % 2
        self.c = dp % 2
        self.yl = t // 8
        self.z = t % 8
        self.dp = dp
        self.t = t

    def dev(self, x=None, yh=None, c=None, yl=None, z=None):
        x = self.x if x is None else x
        yh = self.yh if yh is None else yh
        c = self.c if c is None else c
        yl = self.yl if yl is None else yl
        z = self.z if z is None else z
        return (x * 4 + yh * 2 + c, yl * 8 + z)

    def at_x(self, o):
        return (self.x + o) % 4

    def at_z(self, o):
        return (self.z + o + 8) % 8

    def at_y(self, o):
        y = (self.yh * 2 + self.yl + o) % 4
        return y // 2, y % 2

    def dev_x(self, o):
        return self.dev(x=self.at_x(o))

    def dev_z(self, o):
        return self.dev(z=self.at_z(o))

    def dev_y(self, o):
        yh, yl = self.at_y(o)
        return self.dev(yh=yh, yl=yl)


class Mail:
    def __init__(self, send_sem, recv_sem):
        self.send_sem = send_sem
        self.recv_sem = recv_sem
        self.sent = 0
        self.slots = 0
        self.open = []

    def slot(self, n=1):
        at = self.slots
        self.slots += n
        assert self.slots <= RECVS
        return at

    def send(self, src, dst, slot, device):
        at = self.sent
        self.sent += 1
        assert self.sent <= SENDS
        copy = pltpu.make_async_remote_copy(
            src_ref=src,
            dst_ref=dst,
            send_sem=self.send_sem.at[at],
            recv_sem=self.recv_sem.at[slot],
            device_id=device,
            device_id_type=MESH,
        )
        copy.start()
        self.open.append(copy)

    def wait(self, dst, slot, device):
        pltpu.make_async_remote_copy(
            src_ref=dst,
            dst_ref=dst,
            send_sem=self.send_sem.at[0],
            recv_sem=self.recv_sem.at[slot],
            device_id=device,
            device_id_type=MESH,
        ).wait_recv()

    def finish(self):
        for copy in self.open:
            copy.wait_send()


class Gather:
    def __init__(self, place, mail, block):
        self.p, self.m, self.block = place, mail, block
        self.plus = [mail.slot() for _ in range(4)]
        self.minus = [mail.slot() for _ in range(4)]

    def arrive(self, s):
        p, m = self.p, self.m
        part = (None, None) if s < 4 else (0, 1)
        m.wait(self.block(p.at_z(-s), part[0]), self.plus[s - 1], p.dev_z(1))
        m.wait(self.block(p.at_z(s), part[1]), self.minus[s - 1], p.dev_z(-1))

    def forward(self, s):
        p, m = self.p, self.m
        part = (None, None) if s < 3 else (0, 1)
        low, high = self.block(p.at_z(-s), part[0]), self.block(p.at_z(s), part[1])
        m.send(low, low, self.plus[s], p.dev_z(1))
        m.send(high, high, self.minus[s], p.dev_z(-1))


class Scatter:
    def __init__(self, place, mail, part, rows, out, plus, minus):
        self.p, self.m, self.part, self.rows = place, mail, part, rows
        self.out, self.rp, self.rm = out, plus, minus
        self.plus = [mail.slot() for _ in range(4)]
        self.minus = [mail.slot() for _ in range(4)]

    def step(self, s):
        p, m, rows = self.p, self.m, self.rows
        half = rows // 2
        if s == 0:
            self.out[0] = self.part(0, 0, rows).astype(bf16)
            m.send(self.out.at[0, pl.ds(0, half)], self.rp.at[0, pl.ds(0, half)], self.plus[0], p.dev_z(1))
            m.send(self.out.at[0, pl.ds(half, half)], self.rm.at[0, pl.ds(half, half)], self.minus[0], p.dev_z(-1))
            return
        for way, got, slots, k in ((1, self.rp, self.plus, 2 * s - 1), (-1, self.rm, self.minus, 2 * s)):
            if s == 1:
                lo = 0 if way == 1 else half
                other = half - lo
                m.wait(got.at[0, pl.ds(lo, half)], slots[0], p.dev_z(way))
                self.out[k, lo : lo + half] = (
                    self.part(k, lo, lo + half) + got[0, lo : lo + half].astype(f32)
                ).astype(bf16)
                self.out[k, other : other + half] = self.part(k, other, other + half).astype(bf16)
            else:
                m.wait(got.at[s - 1], slots[s - 1], p.dev_z(way))
                self.out[k] = (self.part(k, 0, rows) + got[s - 1].astype(f32)).astype(bf16)
            m.send(self.out.at[k], got.at[s], slots[s], p.dev_z(way))

    def last(self):
        p, m = self.p, self.m
        m.wait(self.rp.at[3], self.plus[3], p.dev_z(1))
        m.wait(self.rm.at[3], self.minus[3], p.dev_z(-1))
        return self.part(7, 0, self.rows) + self.rp[3].astype(f32) + self.rm[3].astype(f32)


def kernel(
    inputs_hbm, latent, gain, w_latent, w_rope, w_up, kv_hbm, grad_rope,
    gx, gup, glat, grope, ggain,
    inputs, kv, up, nrm, part, ga_out, ga_p, ga_m, gy_out, gy_in, gb_out, gb_p, gb_m, gay_out, gay_in, gnorm,
    wx, wq, wa, wc, intr, ins, pre, pres, gxs,
    rp, rps, gw, gw3, r1, r2, r3z, a1, a2, s3, s3p, s3m, a3x, r3x, ry, rx, a12, r12, a3y, r3y, fin, rfin, glatb, gropeb, gupb,
    gus, gusi, gu, gui, guy, guyi, guz, gn, rgz, rgy, rgx, rgc, gns,
    kv_sem, send_sem, recv_sem,
):
    p = Place()
    m = Mail(send_sem, recv_sem)
    x, yh, c, yl, z = p.x, p.yh, p.c, p.yl, p.z
    sib = p.dev(c=1 - c)
    ylo = p.dev(yl=1 - yl)
    ylo_other = p.dev(yl=1 - yl, c=1 - c)
    yhi = p.dev(yh=1 - yh)
    yhi_other = p.dev(yh=1 - yh, c=1 - c)

    load_inputs = pltpu.make_async_copy(inputs_hbm, inputs, kv_sem.at[1])
    load_inputs.start()
    load_kv = pltpu.make_async_copy(kv_hbm, kv, kv_sem.at[0])
    load_kv.start()

    friends = [sib, ylo_other, yhi_other]
    friends += [p.dev_y(o) for o in (1, 2, 3)] + [p.dev_x(o) for o in (1, 2, 3)]
    friends += [p.dev_z(o) for o in range(1, 8)]
    barrier = pltpu.get_barrier_semaphore()
    for friend in friends:
        pl.semaphore_signal(barrier, inc=1, device_id=friend, device_id_type=MESH)

    lat = latent[...].astype(f32)
    inverse = lax.rsqrt(jnp.mean(lat * lat, axis=-1, keepdims=True) + epsilon)
    normed = lat * inverse * gain[...]
    nrm[yl, z] = normed.T.astype(bf16)
    up[p.dp] = w_up[...]

    y = yh * 2 + yl
    wx[:, 0:512] = w_latent[...]
    wx[:, 512:576] = w_rope[...].T
    wx[:, 576:640] = jnp.zeros((320, 64), bf16)

    def xrows(at):
        return pl.ds(pl.multiple_of(48 * at, 16), 48)

    def yrows(at):
        return pl.ds(pl.multiple_of(192 + 32 * at, 16), 32)

    wa[0:48] = wx[xrows(x)]
    wa[48:80] = wx[yrows(yh * 2 + 1 - yl)]

    @pl.when(c == yl)
    def _():
        wq[z, 0:48] = wx[xrows(x)]
        wq[z, 48:80] = wx[yrows(y)]

    pre[:, 512:576] = grad_rope[...].T
    pre[:, 576:640] = jnp.zeros((128, 64), bf16)
    rp[...] = pre[:, 512:640]

    def turn(i, carry):
        piece = inputs[:, pl.ds(pl.multiple_of(i * 640, 128), 640)].T
        for j in range(2):
            for h in range(2):
                lo = j * 320 + h * 160
                intr[h, 2 * i + j] = piece[lo : lo + 160]
        return carry

    load_inputs.wait()
    lax.fori_loop(0, 8, turn, 0)

    pl.semaphore_wait(barrier, len(friends))

    ux = [m.slot() for _ in range(6)]
    uyh = m.slot()
    usib = [m.slot() for _ in range(8)]

    def ublock(xx, hh, cc):
        return up.at[xx * 4 + hh * 2 + cc]

    mine = ublock(x, yh, c)
    m.send(mine, mine, uyh, yhi)
    for o in (3, 1, 2):
        m.send(mine, mine, ux[o - 1], p.dev_x(o))
    m.send(mine, mine, usib[0], sib)

    def nblock_a(zz, half):
        if half is None:
            return nrm.at[:, zz, pl.ds(0, 256)]
        return nrm.at[half, zz, pl.ds(0, 256)]

    def nblock_b(zz, half):
        if half is None:
            return nrm.at[yl, zz, pl.ds(256, 256)]
        return nrm.at[yl, zz, pl.ds(256 + 128 * half, 128)]

    na = Gather(p, m, nblock_a)
    nb = Gather(p, m, nblock_b)
    nay = m.slot()
    nby = [m.slot() for _ in range(8)]

    def nb_over(zz, slot):
        block = nrm.at[yl, zz, pl.ds(256, 256)]
        m.send(block, block, nby[slot], ylo)

    def nb_arrive(zz, slot):
        m.wait(nrm.at[1 - yl, zz, pl.ds(256, 256)], nby[slot], ylo)

    first = nrm.at[yl, z, pl.ds(0, 256)]
    m.send(first, first, nay, ylo)
    wy = m.slot()
    across = pltpu.make_async_remote_copy(
        src_ref=wa,
        dst_ref=wq.at[z],
        send_sem=send_sem.at[SENDS],
        recv_sem=recv_sem.at[wy],
        device_id=ylo_other,
        device_id_type=MESH,
    )

    nb.forward(0)
    ins_slot = m.slot()
    m.send(intr.at[1 - c], ins, ins_slot, sib)
    rp_slot = m.slot()
    m.send(rp, rps, rp_slot, sib)

    def wblock(zz, half):
        if half is None:
            return wq.at[zz]
        return wq.at[zz, pl.ds(48 * half, 48 - 16 * half)]

    wg = Gather(p, m, wblock)
    offsets = (0, -1, 1, -2, 2, -3, 3, 4)
    onward = {0: 1, -1: 1, -2: 1, -3: 1, 1: 3, 2: 3, 3: 3, 4: 3}
    wslots = {(o, a, d): m.slot() for o in offsets for a in "xy" for d in (1, 3, 2)}

    def wdone(o, a, at):
        zz = p.at_z(o)
        if a == "x":
            return wc.at[zz, xrows((x + at) % 4)]
        return wc.at[zz, yrows((y + at) % 4)]

    def wsend(*which):
        for o in which:
            zz = p.at_z(o)
            for d in (1, 3):
                m.send(wq.at[zz, pl.ds(0, 48)], wdone(o, "x", 0), wslots[o, "x", d], p.dev_x(d))
                m.send(wq.at[zz, pl.ds(48, 32)], wdone(o, "y", 0), wslots[o, "y", d], p.dev_y(d))

    def wonward(*which):
        for o in which:
            for a, dev in (("x", p.dev_x), ("y", p.dev_y)):
                for d in (1, 3):
                    m.wait(wdone(o, a, 4 - d), wslots[o, a, d], dev(d))
                d = onward[o]
                m.send(wdone(o, a, 4 - d), wdone(o, a, 4 - d), wslots[o, a, 2], dev(d))

    def wlast(*which):
        for o in which:
            for a, dev in (("x", p.dev_x), ("y", p.dev_y)):
                m.wait(wdone(o, a, 2), wslots[o, a, 2], dev(onward[o]))
            zz = p.at_z(o)
            wc[zz, xrows(x)] = wq[zz, 0:48]
            wc[zz, yrows(y)] = wq[zz, 48:80]

    m.wait(ublock(x, 1 - yh, c), uyh, yhi)
    theirs = ublock(x, 1 - yh, c)
    for o in (3, 1, 2):
        m.send(theirs, theirs, ux[2 + o], p.dev_x(o))
    m.send(theirs, theirs, usib[1], sib)

    @pl.when(c != yl)
    def _():
        across.start()

    m.wait(nrm.at[1 - yl, z, pl.ds(0, 256)], nay, ylo)
    na.forward(0)
    nb_over(z, 0)

    @pl.when(c != yl)
    def _():
        across.wait_send()
        across.wait_recv()

    wg.forward(0)
    nb.arrive(1)
    nb.forward(1)
    nb_over(p.at_z(-1), 1)
    nb_over(p.at_z(1), 2)
    na.arrive(1)
    na.forward(1)
    wg.arrive(1)
    wg.forward(1)

    def up_arrive(hh, base, *which):
        for o in which:
            theirs = ublock(p.at_x(-o), hh, c)
            m.wait(theirs, ux[base + o], p.dev_x(o))
            m.send(theirs, theirs, usib[2 + base + o], sib)

    def up_across(*which):
        for o in which:
            m.wait(ublock(p.at_x(-o), yh, 1 - c), usib[1 + o], sib)
            m.wait(ublock(p.at_x(-o), 1 - yh, 1 - c), usib[4 + o], sib)

    up_arrive(yh, -1, 3, 1, 2)
    nb.arrive(2)
    nb.forward(2)
    nb_over(p.at_z(-2), 3)
    nb_over(p.at_z(2), 4)
    na.arrive(2)
    na.forward(2)
    load_kv.wait()
    m.wait(ublock(x, yh, 1 - c), usib[0], sib)
    m.wait(ublock(x, 1 - yh, 1 - c), usib[1], sib)
    up_arrive(1 - yh, 2, 3)
    up_across(3)

    def away(k):
        return (z + 8 + (2 * (k % 2) - 1) * (4 - (k + 1) // 2)) % 8

    def compute(k, half):
        rows = kv[:, away(k)].reshape(256, 2048)
        heads = jnp.concatenate(
            [up[pl.ds(4 * p.at_x(2 * half + i), 4)].reshape(128, 2048) for i in range(2)], axis=0
        )
        part[k, :, :, 256 * half : 256 * half + 256] = nt(rows, heads).reshape(2, 128, 256)
        if half == 1:
            gy_out[k] = part[k, 1 - yl, :, 256:512].astype(bf16)

    def part_a(at):
        def get(k, lo, hi):
            return part[k, :, :, 128 * at : 128 * at + 128].reshape(256, 128)[lo:hi]

        return get

    a0 = Scatter(p, m, part_a(0), 256, ga_out.at[0], ga_p.at[0], ga_m.at[0])
    a1s = Scatter(p, m, part_a(1), 256, ga_out.at[1], ga_p.at[1], ga_m.at[1])

    def part_b(k, lo, hi):
        return part[k, yl, lo:hi, 256:512] + gy_in[k, lo:hi].astype(f32)

    by = Scatter(p, m, part_b, 128, gb_out, gb_p, gb_m)
    gys = [m.slot() for _ in range(8)]

    def over(k):
        m.send(gy_out.at[k], gy_in.at[k], gys[k], ylo)

    def over_in(k):
        m.wait(gy_in.at[k], gys[k], ylo)

    m.wait(ins, ins_slot, sib)
    m.wait(rps, rp_slot, sib)

    def part_r(k, lo, hi):
        away = 4 - (k + 1) // 2
        sign = 1 if k % 2 else -1
        zd = (z + 8 + sign * away) % 8
        rope = jnp.concatenate([rp[:, 0:64], rps[:, 0:64]], axis=0)
        none = jnp.zeros((256, 64), bf16)
        low = jnp.concatenate([intr[c, zd], ins[zd]], axis=1)
        high = jnp.concatenate([intr[c, 8 + zd], ins[8 + zd]], axis=1)
        turned = nn(low, jnp.concatenate([rope, none], axis=1)) + nn(high, jnp.concatenate([none, rope], axis=1))
        return turned[lo:hi]

    rs = Scatter(p, m, part_r, 160, s3, s3p, s3m)

    def up_tile(j):
        left = jnp.concatenate([nrm[i // 8, i % 8] for i in range(16)], axis=1)
        right = kv[:, :, :, pl.ds(pl.multiple_of(j * 256, 128), 256)].reshape(2048, 256)
        return nn(left, right)

    def theirs_tile(i, carry):
        gus[i] = up_tile(4 * (1 - c) + i).astype(bf16)
        return carry

    def mine_tile(i, carry):
        gu[:, i] = (up_tile(4 * c + i) + gusi[i].astype(f32)).astype(bf16).reshape(4, 128, 256)
        return carry

    def more(half):
        def body(k, carry):
            compute(k, half)
            return carry

        return body

    compute(0, 0)
    a0.step(0)
    a1s.step(0)
    lax.fori_loop(1, 3, more(0), 0)
    a0.step(1)
    a1s.step(1)
    up_arrive(1 - yh, 2, 1, 2)
    wsend(0, -1, 1)
    up_across(1, 2)
    compute(0, 1)
    over(0)
    lax.fori_loop(1, 3, more(1), 0)
    over(1)
    over(2)
    lax.fori_loop(3, 5, more(0), 0)
    a0.step(2)
    a1s.step(2)
    lax.fori_loop(3, 8, more(1), 0)
    for k in range(3, 8):
        over(k)
    over_in(0)
    by.step(0)
    lax.fori_loop(5, 8, more(0), 0)
    wg.arrive(2)
    wg.forward(2)
    wsend(-2, 2)
    nb.arrive(3)
    nb.forward(3)
    nb_over(p.at_z(-3), 5)
    nb_over(p.at_z(3), 6)
    na.arrive(3)
    na.forward(3)
    a0.step(3)
    a1s.step(3)
    over_in(1)
    over_in(2)
    by.step(1)
    wg.arrive(3)
    wg.forward(3)
    wsend(-3, 3)
    rs.step(0)
    nb.arrive(4)
    nb_over(p.at_z(4), 7)
    over_in(3)
    over_in(4)
    by.step(2)
    gay_slots = [m.slot() for _ in range(2)]
    for i, chain in enumerate((a0, a1s)):
        half_a = chain.last().reshape(2, 128, 128)
        gay_out[i] = half_a.astype(bf16)
        m.send(gay_out.at[i, 1 - yl], gay_in.at[i], gay_slots[i], ylo)
        for h in range(2):
            part[0, h, :, 128 * i : 128 * i + 128] = half_a[h]
    na.arrive(4)
    wg.arrive(4)
    wsend(4)
    rs.step(1)
    over_in(5)
    over_in(6)
    by.step(3)
    wonward(0, -1, 1)
    over_in(7)
    part[0, 0, :, 256:512] = by.last()
    for i in range(2):
        m.wait(gay_in.at[i], gay_slots[i], ylo)
    own_a = part[0, yl, :, 0:256] + jnp.concatenate([gay_in[0], gay_in[1]], axis=1).astype(f32)
    for i in range(2):
        gnorm[:, pl.ds(pl.multiple_of(128 * p.at_x(i), 128), 128)] = own_a[:, 128 * i : 128 * i + 128]
        gnorm[:, pl.ds(pl.multiple_of(128 * p.at_x(2 + i), 128), 128)] = part[0, 0, :, 256 + 128 * i : 384 + 128 * i]
    grad_norm = gnorm[...]
    lat = latent[...].astype(f32)
    inverse = lax.rsqrt(jnp.mean(lat * lat, axis=-1, keepdims=True) + epsilon)
    scaled = grad_norm * gain[...]
    inner = jnp.mean(scaled * lat, axis=-1, keepdims=True)
    pre[:, 0:512] = (inverse * scaled - lat * (inverse * inverse * inverse) * inner).astype(bf16)
    pre_slot = m.slot()
    m.send(pre, pres, pre_slot, sib)
    gsum = jnp.sum(grad_norm * lat * inverse, axis=0, keepdims=True)
    gn[...] = jnp.zeros((8, 128), f32)
    for q in range(4):
        gn[q : q + 1, :] = gsum[:, 128 * q : 128 * q + 128]
    rgz_slots = [m.slot() for _ in range(7)]
    for o in range(1, 8):
        m.send(gn, rgz.at[o - 1], rgz_slots[o - 1], p.dev_z(o))

    m.wait(pres, pre_slot, sib)
    both = jnp.concatenate([pre[...], pres[...]], axis=0)

    def gw_tile(i, carry):
        at = pl.ds(4 * i, 4)
        left = jnp.concatenate(
            [intr[c, at].reshape(640, 128), ins[at].reshape(640, 128)], axis=1
        )
        got = nn(left, both[:, 0:512]).astype(bf16)
        for q in range(4):
            piece = got[:, 128 * q : 128 * q + 128].reshape(4, 160, 128)
            gw[q, at] = piece[:, 0:128]
            for j in range(4):
                gw3[4 * (i % 2) + j, q, i // 2] = piece[j, 128:160]
        return carry

    lax.fori_loop(0, 4, gw_tile, 0)
    r3z_slots = [m.slot() for _ in range(7)]
    for o in (4, 3, 5, 2, 6, 1, 7):
        m.send(gw3.at[p.at_z(o)], r3z.at[o - 1], r3z_slots[o - 1], p.dev_z(o))
    r1_slots = [m.slot() for _ in range(3)]
    r2_slots = [m.slot() for _ in range(3)]
    for o in (2, 1, 3):
        m.send(gw.at[p.at_x(o), :, pl.ds(0, 64)], r1.at[o - 1], r1_slots[o - 1], p.dev_x(o))
        hh, ll = p.at_y(o)
        m.send(
            gw.at[:, pl.ds(8 * ll, 8), pl.ds(pl.multiple_of(64 + 32 * hh, 16), 32)],
            r2.at[o - 1], r2_slots[o - 1], p.dev_y(o),
        )

    for i, o in enumerate((0, -1, 1, -2, 2, -3, 3, 4)):
        nb_arrive(p.at_z(o), i)
    lax.fori_loop(0, 4, theirs_tile, 0)
    gus_slot = m.slot()
    m.send(gus, gusi, gus_slot, sib)
    m.wait(gusi, gus_slot, sib)
    lax.fori_loop(0, 4, mine_tile, 0)
    gux = [m.slot() for _ in range(3)]
    for o in (1, 3, 2):
        m.send(gu.at[p.at_x(o)], gui.at[o - 1], gux[o - 1], p.dev_x(o))
    rs.step(2)
    wonward(-2, 2, -3, 3, 4)
    rs.step(3)
    turned = rs.last().astype(bf16)
    for o in (1, 7, 2, 6, 3, 5, 4):
        m.wait(r3z.at[o - 1], r3z_slots[o - 1], p.dev_z(o))
    for q in range(4):
        sum3 = gw3[z, q].astype(f32)
        for o in range(7):
            sum3 = sum3 + r3z[o, q].astype(f32)
        a3x[q, 0:64] = sum3.reshape(64, 128).astype(bf16)
        a3x[q, 64:224] = turned
    r3x_slots = [m.slot() for _ in range(3)]
    for o in (2, 1, 3):
        m.send(a3x.at[p.at_x(o)], r3x.at[o - 1], r3x_slots[o - 1], p.dev_x(o))

    for o in range(1, 8):
        m.wait(rgz.at[o - 1], rgz_slots[o - 1], p.dev_z(o))
    gns[0] = gn[...] + jnp.sum(rgz[...], axis=0)
    rgy_slots = [m.slot() for _ in range(3)]
    for o in (1, 2, 3):
        m.send(gns.at[0], rgy.at[o - 1], rgy_slots[o - 1], p.dev_y(o))

    for o in (1, 3, 2):
        m.wait(r1.at[o - 1], r1_slots[o - 1], p.dev_x(o))
    for h in range(2):
        rows = pl.ds(32 * h, 32)
        sum1 = gw[x, :, rows].astype(f32)
        for o in range(3):
            sum1 = sum1 + r1[o, :, rows].astype(f32)
        a1[h] = sum1.astype(bf16)
    ry_slots = [m.slot() for _ in range(3)]
    for o in (2, 1, 3):
        hh, ll = p.at_y(o)
        m.send(a1.at[hh, pl.ds(8 * ll, 8)], ry.at[o - 1], ry_slots[o - 1], p.dev_y(o))
    for o in (1, 3, 2):
        m.wait(r2.at[o - 1], r2_slots[o - 1], p.dev_y(o))
    for q in range(4):
        sum2 = gw[q, pl.ds(8 * yl, 8), pl.ds(pl.multiple_of(64 + 32 * yh, 16), 32)].astype(f32)
        for o in range(3):
            sum2 = sum2 + r2[o, q].astype(f32)
        a2[q] = sum2.astype(bf16)
    rx_slots = [m.slot() for _ in range(3)]
    for o in (2, 1, 3):
        m.send(a2.at[p.at_x(o)], rx.at[o - 1], rx_slots[o - 1], p.dev_x(o))

    for o in (1, 2, 3):
        m.wait(rgy.at[o - 1], rgy_slots[o - 1], p.dev_y(o))
    gns[1] = gns[0] + rgy[0] + rgy[1] + rgy[2]
    rgx_slots = [m.slot() for _ in range(3)]
    for o in (1, 2, 3):
        m.send(gns.at[1], rgx.at[o - 1], rgx_slots[o - 1], p.dev_x(o))

    for o in (1, 3, 2):
        m.wait(r3x.at[o - 1], r3x_slots[o - 1], p.dev_x(o))
    sum3 = a3x[x].astype(f32) + r3x[0].astype(f32) + r3x[1].astype(f32) + r3x[2].astype(f32)
    for ll in range(2):
        for hh in range(2):
            lo = 32 * ll + 16 * hh
            a3y[2 * hh + ll, 0:16] = sum3[lo : lo + 16].astype(bf16)
            a3y[2 * hh + ll, 16:176] = sum3[64:224].astype(bf16)
    r3y_slots = [m.slot() for _ in range(3)]
    for o in (2, 1, 3):
        hh, ll = p.at_y(o)
        m.send(a3y.at[2 * hh + ll], r3y.at[o - 1], r3y_slots[o - 1], p.dev_y(o))

    wlast(0, -1, 1, -2, 2, -3, 3, 4)

    own_columns = pl.multiple_of(2560 * c, 128)

    def gx_tile(i, carry):
        got = nt(both, wc[pl.ds(2 * i, 2)].reshape(640, 640)).astype(bf16)
        gx[:, pl.ds(pl.multiple_of(own_columns + i * 640, 128), 640)] = got[0:128]
        gxs[:, pl.ds(pl.multiple_of(i * 640, 128), 640)] = got[128:256]
        return carry

    lax.fori_loop(0, 4, gx_tile, 0)
    gx_slot = m.slot()
    m.send(gxs, gx.at[:, pl.ds(own_columns, 2560)], gx_slot, sib)
    for o in (1, 3, 2):
        m.wait(ry.at[o - 1], ry_slots[o - 1], p.dev_y(o))
    sum1 = a1[yh, pl.ds(8 * yl, 8)].astype(f32)
    for o in range(3):
        sum1 = sum1 + ry[o].astype(f32)
    a12[:, 0:32] = sum1.astype(bf16)
    for o in (1, 3, 2):
        m.wait(rx.at[o - 1], rx_slots[o - 1], p.dev_x(o))
    sum2 = a2[x].astype(f32)
    for o in range(3):
        sum2 = sum2 + rx[o].astype(f32)
    a12[:, 32:64] = sum2.astype(bf16)
    r12_slots = [m.slot() for _ in range(7)]
    for o in range(1, 8):
        m.send(a12.at[p.at_z(o)], r12.at[o - 1], r12_slots[o - 1], p.dev_z(o))

    for o in (1, 3, 2):
        m.wait(gui.at[o - 1], gux[o - 1], p.dev_x(o))
    for h in range(2):
        rows = pl.ds(64 * h, 64)
        total = gu[x, :, rows].astype(f32)
        for o in range(3):
            total = total + gui[o, :, rows].astype(f32)
        guy[h] = total.astype(bf16)
    guy_slot = m.slot()
    m.send(guy.at[1 - yh], guyi, guy_slot, yhi)

    m.wait(guyi, guy_slot, yhi)
    total = guy[yh].astype(f32) + guyi[...].astype(f32)
    for h in range(2):
        guz[h] = total[:, 32 * h : 32 * h + 32].astype(bf16)
    guz_slot = m.slot()
    m.send(guz.at[1 - c], gupb, guz_slot, sib)
    for i in range(4):
        gup[:, pl.ds(pl.multiple_of(1024 * c + 256 * i, 128), 256)] = guz[c, i]

    for o in (1, 2, 3):
        m.wait(rgx.at[o - 1], rgx_slots[o - 1], p.dev_x(o))
    gns[2] = gns[1] + rgx[0] + rgx[1] + rgx[2]
    rgc_slot = m.slot()
    m.send(gns.at[2], rgc, rgc_slot, sib)

    for o in (1, 2, 3):
        m.wait(r3y.at[o - 1], r3y_slots[o - 1], p.dev_y(o))
    sum3 = a3y[2 * yh + yl].astype(f32) + r3y[0].astype(f32) + r3y[1].astype(f32) + r3y[2].astype(f32)
    fin[64:80] = sum3[0:16].astype(bf16)
    rfin[...] = sum3[16:176].astype(bf16)
    rfin_slot = m.slot()
    m.send(rfin, gropeb.at[c], rfin_slot, sib)
    gropeb[c] = rfin[...]
    for o in range(1, 8):
        m.wait(r12.at[o - 1], r12_slots[o - 1], p.dev_z(o))
    fin[0:64] = (a12[z].astype(f32) + jnp.sum(r12[...].astype(f32), axis=0)).astype(bf16)
    fin_slots = [m.slot() for _ in range(3)]
    for slot, friend in zip(fin_slots, (sib, yhi, yhi_other)):
        m.send(fin, glatb.at[c, yh], slot, friend)
    glatb[c, yh] = fin[...]

    m.wait(rgc, rgc_slot, sib)
    total = gns[2] + rgc[...]
    for q in range(4):
        ggain[:, 128 * q : 128 * q + 128] = total[q : q + 1]
    m.wait(gupb, guz_slot, sib)
    for i in range(4):
        gup[:, pl.ds(pl.multiple_of(1024 * (1 - c) + 256 * i, 128), 256)] = gupb[i]

    def columns(first, n, rows):
        row = lax.broadcasted_iota(jnp.int32, (n, 128), 0)
        column = lax.broadcasted_iota(jnp.int32, (n, 128), 1)
        return nt((column == row + first).astype(bf16), rows).astype(bf16)

    m.wait(gropeb.at[1 - c], rfin_slot, sib)
    grope[...] = columns(yl * 64 + p.dp * 4, 16, gropeb[...].reshape(320, 128))[0:4]
    m.wait(glatb.at[1 - c, yh], fin_slots[0], sib)
    m.wait(glatb.at[c, 1 - yh], fin_slots[1], yhi)
    m.wait(glatb.at[1 - c, 1 - yh], fin_slots[2], yhi_other)
    rows = []
    for h in range(2):
        for lo, n in ((0, 32), (32, 32), (64, 16)):
            for i in range(2):
                rows.append(glatb[h, i, lo : lo + n])
    glat[...] = columns((p.dp % 4) * 32, 32, jnp.concatenate(rows, axis=0))
    m.wait(gx.at[:, pl.ds(pl.multiple_of(2560 * (1 - c), 128), 2560)], gx_slot, sib)
    m.finish()


def shards(inputs, latent, gain, w_latent, w_rope, w_up, grad_kv, grad_rope):
    V = lambda *shape: pltpu.VMEM(shape, bf16)
    F = lambda *shape: pltpu.VMEM(shape, f32)
    whole = pl.BlockSpec(memory_space=pltpu.VMEM)
    scratch = dict(
        inputs=V(128, 5120), kv=V(2, 8, 128, 2048), up=V(16, 32, 2048), nrm=V(2, 8, 512, 128), part=F(8, 2, 128, 512),
        ga_out=V(2, 8, 256, 128), ga_p=V(2, 4, 256, 128), ga_m=V(2, 4, 256, 128),
        gy_out=V(8, 128, 256), gy_in=V(8, 128, 256),
        gb_out=V(8, 128, 256), gb_p=V(4, 128, 256), gb_m=V(4, 128, 256),
        gay_out=V(2, 2, 128, 128), gay_in=V(2, 128, 128), gnorm=F(128, 512),
        wx=V(320, 640), wq=V(8, 80, 640), wa=V(80, 640), wc=V(8, 320, 640), intr=V(2, 16, 160, 128), ins=V(16, 160, 128),
        pre=V(128, 640), pres=V(128, 640), gxs=V(128, 2560),
        rp=V(128, 128), rps=V(128, 128), gw=V(4, 16, 128, 128), gw3=V(8, 4, 2, 32, 128), r1=V(3, 16, 64, 128), r2=V(3, 4, 8, 32, 128), r3z=V(7, 4, 2, 32, 128),
        a1=V(2, 16, 32, 128), a2=V(4, 8, 32, 128),
        s3=V(8, 160, 128), s3p=V(4, 160, 128), s3m=V(4, 160, 128),
        a3x=V(4, 224, 128), r3x=V(3, 224, 128), ry=V(3, 8, 32, 128), rx=V(3, 8, 32, 128),
        a12=V(8, 64, 128), r12=V(7, 64, 128), a3y=V(4, 176, 128), r3y=V(3, 176, 128),
        fin=V(80, 128), rfin=V(160, 128), glatb=V(2, 2, 80, 128), gropeb=V(2, 160, 128), gupb=V(4, 32, 256),
        gus=V(4, 512, 256), gusi=V(4, 512, 256), gu=V(4, 4, 128, 256), gui=V(3, 4, 128, 256),
        guy=V(2, 4, 64, 256), guyi=V(4, 64, 256), guz=V(2, 4, 32, 256),
        gn=F(8, 128), rgz=F(7, 8, 128), rgy=F(3, 8, 128), rgx=F(3, 8, 128), rgc=F(8, 128), gns=F(3, 8, 128),
        kv_sem=pltpu.SemaphoreType.DMA((2,)),
        send_sem=pltpu.SemaphoreType.DMA((SENDS + 1,)),
        recv_sem=pltpu.SemaphoreType.DMA((RECVS,)),
    )

    def body(*refs):
        own = refs[:13]
        kernel(*own, **dict(zip(scratch, refs[13:])))

    gx, gup, glat, grope, ggain = pl.pallas_call(
        body,
        out_shape=(
            jax.ShapeDtypeStruct((128, 5120), bf16),
            jax.ShapeDtypeStruct((32, 2048), bf16),
            jax.ShapeDtypeStruct((32, 320), bf16),
            jax.ShapeDtypeStruct((4, 320), bf16),
            jax.ShapeDtypeStruct((1, 512), f32),
        ),
        in_specs=[pl.BlockSpec(memory_space=pl.ANY)] + [whole] * 5 + [pl.BlockSpec(memory_space=pl.ANY), whole],
        out_specs=(whole,) * 5,
        scratch_shapes=list(scratch.values()),
        compiler_params=pltpu.CompilerParams(
            collective_id=0, has_side_effects=True, vmem_limit_bytes=60 << 20
        ),
    )(
        inputs, latent, gain.reshape(1, 512), w_latent, w_rope.T, w_up,
        grad_kv.reshape(2, 8, 128, 2048), grad_rope.T,
    )

    def hand_over(*refs):
        for i in range(5):
            refs[5 + i][...] = refs[i][...]

    made = (gx, gup, glat, grope, ggain)
    gx, gup, glat, grope, ggain = pl.pallas_call(
        hand_over,
        out_shape=tuple(jax.ShapeDtypeStruct(a.shape, a.dtype) for a in made),
        in_specs=[whole] * 5,
        out_specs=(whole,) * 5,
    )(*made)
    return gx, gup, glat.T, grope.T, ggain.reshape(512)


def solution(mesh):
    in_specs = (
        P(("dp", "tensor"), None),
        P(("dp", "tensor"), None),
        P(),
        P("tensor", None),
        P("tensor", None),
        P("dp", "tensor"),
        P("dp", "tensor"),
        P(("dp", "tensor"), None),
    )
    out_specs = (
        P(("dp", "tensor"), None),
        P("dp", "tensor"),
        P("tensor", "dp"),
        P("tensor", "dp"),
        P(),
    )
    return jax.shard_map(shards, mesh=mesh, in_specs=in_specs, out_specs=out_specs, check_vma=False)
```

```python
import jax
import jax.numpy as jnp
from jax import lax
from jax.experimental import pallas as pl
from jax.experimental.pallas import tpu as pltpu
from jax.sharding import PartitionSpec as P

MESH = pl.DeviceIdType.MESH
epsilon = 1e-06
f32 = jnp.float32
bf16 = jnp.bfloat16

SENDS = 260
RECVS = 260


def nt(a, b):
    return lax.dot_general(a, b, (((1,), (1,)), ((), ())), preferred_element_type=f32)


def nn(a, b):
    return lax.dot_general(a, b, (((1,), (0,)), ((), ())), preferred_element_type=f32)


class Place:
    def __init__(self):
        dp = lax.axis_index("dp")
        t = lax.axis_index("tensor")
        self.x = dp // 4
        self.yh = (dp // 2) % 2
        self.c = dp % 2
        self.yl = t // 8
        self.z = t % 8
        self.dp = dp
        self.t = t

    def dev(self, x=None, yh=None, c=None, yl=None, z=None):
        x = self.x if x is None else x
        yh = self.yh if yh is None else yh
        c = self.c if c is None else c
        yl = self.yl if yl is None else yl
        z = self.z if z is None else z
        return (x * 4 + yh * 2 + c, yl * 8 + z)

    def at_x(self, o):
        return (self.x + o) % 4

    def at_z(self, o):
        return (self.z + o + 8) % 8

    def at_y(self, o):
        y = (self.yh * 2 + self.yl + o) % 4
        return y // 2, y % 2

    def dev_x(self, o):
        return self.dev(x=self.at_x(o))

    def dev_z(self, o):
        return self.dev(z=self.at_z(o))

    def dev_y(self, o):
        yh, yl = self.at_y(o)
        return self.dev(yh=yh, yl=yl)


class Mail:
    def __init__(self, send_sem, recv_sem):
        self.send_sem = send_sem
        self.recv_sem = recv_sem
        self.sent = 0
        self.slots = 0
        self.open = []

    def slot(self, n=1):
        at = self.slots
        self.slots += n
        assert self.slots <= RECVS
        return at

    def send(self, src, dst, slot, device):
        at = self.sent
        self.sent += 1
        assert self.sent <= SENDS
        copy = pltpu.make_async_remote_copy(
            src_ref=src,
            dst_ref=dst,
            send_sem=self.send_sem.at[at],
            recv_sem=self.recv_sem.at[slot],
            device_id=device,
            device_id_type=MESH,
        )
        copy.start()
        self.open.append(copy)

    def wait(self, dst, slot, device):
        pltpu.make_async_remote_copy(
            src_ref=dst,
            dst_ref=dst,
            send_sem=self.send_sem.at[0],
            recv_sem=self.recv_sem.at[slot],
            device_id=device,
            device_id_type=MESH,
        ).wait_recv()

    def finish(self):
        for copy in self.open:
            copy.wait_send()


class Gather:
    def __init__(self, place, mail, block):
        self.p, self.m, self.block = place, mail, block
        self.plus = [mail.slot() for _ in range(4)]
        self.minus = [mail.slot() for _ in range(4)]

    def arrive(self, s):
        p, m = self.p, self.m
        part = (None, None) if s < 4 else (0, 1)
        m.wait(self.block(p.at_z(-s), part[0]), self.plus[s - 1], p.dev_z(1))
        m.wait(self.block(p.at_z(s), part[1]), self.minus[s - 1], p.dev_z(-1))

    def forward(self, s):
        p, m = self.p, self.m
        part = (None, None) if s < 3 else (0, 1)
        low, high = self.block(p.at_z(-s), part[0]), self.block(p.at_z(s), part[1])
        m.send(low, low, self.plus[s], p.dev_z(1))
        m.send(high, high, self.minus[s], p.dev_z(-1))


class Scatter:
    def __init__(self, place, mail, part, rows, out, plus, minus):
        self.p, self.m, self.part, self.rows = place, mail, part, rows
        self.out, self.rp, self.rm = out, plus, minus
        self.plus = [mail.slot() for _ in range(4)]
        self.minus = [mail.slot() for _ in range(4)]

    def step(self, s):
        p, m, rows = self.p, self.m, self.rows
        half = rows // 2
        if s == 0:
            self.out[0] = self.part(0, 0, rows).astype(bf16)
            m.send(self.out.at[0, pl.ds(0, half)], self.rp.at[0, pl.ds(0, half)], self.plus[0], p.dev_z(1))
            m.send(self.out.at[0, pl.ds(half, half)], self.rm.at[0, pl.ds(half, half)], self.minus[0], p.dev_z(-1))
            return
        for way, got, slots, k in ((1, self.rp, self.plus, 2 * s - 1), (-1, self.rm, self.minus, 2 * s)):
            if s == 1:
                lo = 0 if way == 1 else half
                other = half - lo
                m.wait(got.at[0, pl.ds(lo, half)], slots[0], p.dev_z(way))
                self.out[k, lo : lo + half] = (
                    self.part(k, lo, lo + half) + got[0, lo : lo + half].astype(f32)
                ).astype(bf16)
                self.out[k, other : other + half] = self.part(k, other, other + half).astype(bf16)
            else:
                m.wait(got.at[s - 1], slots[s - 1], p.dev_z(way))
                self.out[k] = (self.part(k, 0, rows) + got[s - 1].astype(f32)).astype(bf16)
            m.send(self.out.at[k], got.at[s], slots[s], p.dev_z(way))

    def last(self):
        p, m = self.p, self.m
        m.wait(self.rp.at[3], self.plus[3], p.dev_z(1))
        m.wait(self.rm.at[3], self.minus[3], p.dev_z(-1))
        return self.part(7, 0, self.rows) + self.rp[3].astype(f32) + self.rm[3].astype(f32)


def kernel(
    inputs_hbm, latent, gain, w_latent, w_rope, w_up, kv_hbm, grad_rope,
    gx, gup, glat, grope, ggain,
    inputs, kv, up, nrm, part, ga_out, ga_p, ga_m, gy_out, gy_in, gb_out, gb_p, gb_m, gay_out, gay_in, gnorm,
    wx, wq, wa, wc, intr, ins, pre, pres, gxs,
    rp, rps, gw, gw3, r1, r2, r3z, a1, a2, s3, s3p, s3m, a3x, r3x, ry, rx, a12, r12, a3y, r3y, fin, rfin, glatb, gropeb, gupb,
    gus, gusi, gu, gui, guy, guyi, guz, gn, rgz, rgy, rgx, rgc, gns,
    kv_sem, send_sem, recv_sem,
):
    p = Place()
    m = Mail(send_sem, recv_sem)
    x, yh, c, yl, z = p.x, p.yh, p.c, p.yl, p.z
    sib = p.dev(c=1 - c)
    ylo = p.dev(yl=1 - yl)
    ylo_other = p.dev(yl=1 - yl, c=1 - c)
    yhi = p.dev(yh=1 - yh)
    yhi_other = p.dev(yh=1 - yh, c=1 - c)

    load_inputs = pltpu.make_async_copy(inputs_hbm, inputs, kv_sem.at[1])
    load_inputs.start()
    load_kv = pltpu.make_async_copy(kv_hbm, kv, kv_sem.at[0])
    load_kv.start()

    friends = [sib, ylo_other, yhi_other]
    friends += [p.dev_y(o) for o in (1, 2, 3)] + [p.dev_x(o) for o in (1, 2, 3)]
    friends += [p.dev_z(o) for o in range(1, 8)]
    barrier = pltpu.get_barrier_semaphore()
    for friend in friends:
        pl.semaphore_signal(barrier, inc=1, device_id=friend, device_id_type=MESH)

    lat = latent[...].astype(f32)
    inverse = lax.rsqrt(jnp.mean(lat * lat, axis=-1, keepdims=True) + epsilon)
    normed = lat * inverse * gain[...]
    nrm[yl, z] = normed.T.astype(bf16)
    up[p.dp] = w_up[...]

    y = yh * 2 + yl
    wx[:, 0:512] = w_latent[...]
    wx[:, 512:576] = w_rope[...].T
    wx[:, 576:640] = jnp.zeros((320, 64), bf16)

    def xrows(at):
        return pl.ds(pl.multiple_of(48 * at, 16), 48)

    def yrows(at):
        return pl.ds(pl.multiple_of(192 + 32 * at, 16), 32)

    wa[0:48] = wx[xrows(x)]
    wa[48:80] = wx[yrows(yh * 2 + 1 - yl)]

    @pl.when(c == yl)
    def _():
        wq[z, 0:48] = wx[xrows(x)]
        wq[z, 48:80] = wx[yrows(y)]

    pre[:, 512:576] = grad_rope[...].T
    pre[:, 576:640] = jnp.zeros((128, 64), bf16)
    rp[...] = pre[:, 512:640]

    def turn(i, carry):
        piece = inputs[:, pl.ds(pl.multiple_of(i * 640, 128), 640)].T
        for j in range(2):
            for h in range(2):
                lo = j * 320 + h * 160
                intr[h, 2 * i + j] = piece[lo : lo + 160]
        return carry

    load_inputs.wait()
    lax.fori_loop(0, 8, turn, 0)

    pl.semaphore_wait(barrier, len(friends))

    ux = [m.slot() for _ in range(6)]
    uyh = m.slot()
    usib = [m.slot() for _ in range(8)]

    def ublock(xx, hh, cc):
        return up.at[xx * 4 + hh * 2 + cc]

    mine = ublock(x, yh, c)
    m.send(mine, mine, uyh, yhi)
    for o in (3, 1, 2):
        m.send(mine, mine, ux[o - 1], p.dev_x(o))
    m.send(mine, mine, usib[0], sib)

    def nblock_a(zz, half):
        if half is None:
            return nrm.at[:, zz, pl.ds(0, 256)]
        return nrm.at[half, zz, pl.ds(0, 256)]

    def nblock_b(zz, half):
        if half is None:
            return nrm.at[yl, zz, pl.ds(256, 256)]
        return nrm.at[yl, zz, pl.ds(256 + 128 * half, 128)]

    na = Gather(p, m, nblock_a)
    nb = Gather(p, m, nblock_b)
    nay = m.slot()
    nby = [m.slot() for _ in range(8)]

    def nb_over(zz, slot):
        block = nrm.at[yl, zz, pl.ds(256, 256)]
        m.send(block, block, nby[slot], ylo)

    def nb_arrive(zz, slot):
        m.wait(nrm.at[1 - yl, zz, pl.ds(256, 256)], nby[slot], ylo)

    first = nrm.at[yl, z, pl.ds(0, 256)]
    m.send(first, first, nay, ylo)
    wy = m.slot()
    across = pltpu.make_async_remote_copy(
        src_ref=wa,
        dst_ref=wq.at[z],
        send_sem=send_sem.at[SENDS],
        recv_sem=recv_sem.at[wy],
        device_id=ylo_other,
        device_id_type=MESH,
    )

    nb.forward(0)
    ins_slot = m.slot()
    m.send(intr.at[1 - c], ins, ins_slot, sib)
    rp_slot = m.slot()
    m.send(rp, rps, rp_slot, sib)

    def wblock(zz, half):
        if half is None:
            return wq.at[zz]
        return wq.at[zz, pl.ds(48 * half, 48 - 16 * half)]

    wg = Gather(p, m, wblock)
    offsets = (0, -1, 1, -2, 2, -3, 3, 4)
    onward = {0: 1, -1: 1, -2: 1, -3: 1, 1: 3, 2: 3, 3: 3, 4: 3}
    wslots = {(o, a, d): m.slot() for o in offsets for a in "xy" for d in (1, 3, 2)}

    def wdone(o, a, at):
        zz = p.at_z(o)
        if a == "x":
            return wc.at[zz, xrows((x + at) % 4)]
        return wc.at[zz, yrows((y + at) % 4)]

    def wsend(*which):
        for o in which:
            zz = p.at_z(o)
            for d in (1, 3):
                m.send(wq.at[zz, pl.ds(0, 48)], wdone(o, "x", 0), wslots[o, "x", d], p.dev_x(d))
                m.send(wq.at[zz, pl.ds(48, 32)], wdone(o, "y", 0), wslots[o, "y", d], p.dev_y(d))

    def wonward(*which):
        for o in which:
            for a, dev in (("x", p.dev_x), ("y", p.dev_y)):
                for d in (1, 3):
                    m.wait(wdone(o, a, 4 - d), wslots[o, a, d], dev(d))
                d = onward[o]
                m.send(wdone(o, a, 4 - d), wdone(o, a, 4 - d), wslots[o, a, 2], dev(d))

    def wlast(*which):
        for o in which:
            for a, dev in (("x", p.dev_x), ("y", p.dev_y)):
                m.wait(wdone(o, a, 2), wslots[o, a, 2], dev(onward[o]))
            zz = p.at_z(o)
            wc[zz, xrows(x)] = wq[zz, 0:48]
            wc[zz, yrows(y)] = wq[zz, 48:80]

    m.wait(ublock(x, 1 - yh, c), uyh, yhi)
    theirs = ublock(x, 1 - yh, c)
    for o in (3, 1, 2):
        m.send(theirs, theirs, ux[2 + o], p.dev_x(o))
    m.send(theirs, theirs, usib[1], sib)

    @pl.when(c != yl)
    def _():
        across.start()

    m.wait(nrm.at[1 - yl, z, pl.ds(0, 256)], nay, ylo)
    na.forward(0)
    nb_over(z, 0)

    @pl.when(c != yl)
    def _():
        across.wait_send()
        across.wait_recv()

    wg.forward(0)
    nb.arrive(1)
    nb.forward(1)
    nb_over(p.at_z(-1), 1)
    nb_over(p.at_z(1), 2)
    na.arrive(1)
    na.forward(1)
    wg.arrive(1)
    wg.forward(1)

    def up_arrive(hh, base, *which):
        for o in which:
            theirs = ublock(p.at_x(-o), hh, c)
            m.wait(theirs, ux[base + o], p.dev_x(o))
            m.send(theirs, theirs, usib[2 + base + o], sib)

    def up_across(*which):
        for o in which:
            m.wait(ublock(p.at_x(-o), yh, 1 - c), usib[1 + o], sib)
            m.wait(ublock(p.at_x(-o), 1 - yh, 1 - c), usib[4 + o], sib)

    up_arrive(yh, -1, 3, 1, 2)
    wg.arrive(2)
    wg.forward(2)
    load_kv.wait()
    m.wait(ublock(x, yh, 1 - c), usib[0], sib)
    m.wait(ublock(x, 1 - yh, 1 - c), usib[1], sib)
    up_arrive(1 - yh, 2, 3)
    up_across(3)

    def away(k):
        return (z + 8 + (2 * (k % 2) - 1) * (4 - (k + 1) // 2)) % 8

    def compute(k, half):
        rows = kv[:, away(k)].reshape(256, 2048)
        heads = jnp.concatenate(
            [up[pl.ds(4 * p.at_x(2 * half + i), 4)].reshape(128, 2048) for i in range(2)], axis=0
        )
        part[k, :, :, 256 * half : 256 * half + 256] = nt(rows, heads).reshape(2, 128, 256)
        if half == 1:
            gy_out[k] = part[k, 1 - yl, :, 256:512].astype(bf16)

    def part_a(at):
        def get(k, lo, hi):
            return part[k, :, :, 128 * at : 128 * at + 128].reshape(256, 128)[lo:hi]

        return get

    a0 = Scatter(p, m, part_a(0), 256, ga_out.at[0], ga_p.at[0], ga_m.at[0])
    a1s = Scatter(p, m, part_a(1), 256, ga_out.at[1], ga_p.at[1], ga_m.at[1])

    def part_b(k, lo, hi):
        return part[k, yl, lo:hi, 256:512] + gy_in[k, lo:hi].astype(f32)

    by = Scatter(p, m, part_b, 128, gb_out, gb_p, gb_m)
    gys = [m.slot() for _ in range(8)]

    def over(k):
        m.send(gy_out.at[k], gy_in.at[k], gys[k], ylo)

    def over_in(k):
        m.wait(gy_in.at[k], gys[k], ylo)

    m.wait(ins, ins_slot, sib)
    m.wait(rps, rp_slot, sib)

    def part_r(k, lo, hi):
        away = 4 - (k + 1) // 2
        sign = 1 if k % 2 else -1
        zd = (z + 8 + sign * away) % 8
        rope = jnp.concatenate([rp[:, 0:64], rps[:, 0:64]], axis=0)
        none = jnp.zeros((256, 64), bf16)
        low = jnp.concatenate([intr[c, zd], ins[zd]], axis=1)
        high = jnp.concatenate([intr[c, 8 + zd], ins[8 + zd]], axis=1)
        turned = nn(low, jnp.concatenate([rope, none], axis=1)) + nn(high, jnp.concatenate([none, rope], axis=1))
        return turned[lo:hi]

    rs = Scatter(p, m, part_r, 160, s3, s3p, s3m)

    def up_tile(j):
        left = jnp.concatenate([nrm[i // 8, i % 8] for i in range(16)], axis=1)
        right = kv[:, :, :, pl.ds(pl.multiple_of(j * 256, 128), 256)].reshape(2048, 256)
        return nn(left, right)

    def theirs_tile(i, carry):
        gus[i] = up_tile(4 * (1 - c) + i).astype(bf16)
        return carry

    def mine_tile(i, carry):
        gu[:, i] = (up_tile(4 * c + i) + gusi[i].astype(f32)).astype(bf16).reshape(4, 128, 256)
        return carry

    def more(half):
        def body(k, carry):
            compute(k, half)
            return carry

        return body

    compute(0, 0)
    a0.step(0)
    a1s.step(0)
    lax.fori_loop(1, 3, more(0), 0)
    a0.step(1)
    a1s.step(1)
    up_arrive(1 - yh, 2, 1, 2)
    wsend(0, -1, 1)
    up_across(1, 2)
    compute(0, 1)
    over(0)
    lax.fori_loop(1, 3, more(1), 0)
    over(1)
    over(2)
    lax.fori_loop(3, 5, more(0), 0)
    a0.step(2)
    a1s.step(2)
    wg.arrive(3)
    wg.forward(3)
    wsend(-2, 2, -3, 3)
    lax.fori_loop(3, 8, more(1), 0)
    for k in range(3, 8):
        over(k)
    over_in(0)
    by.step(0)
    lax.fori_loop(5, 8, more(0), 0)
    a0.step(3)
    a1s.step(3)
    over_in(1)
    over_in(2)
    by.step(1)
    nb.arrive(2)
    nb.forward(2)
    nb_over(p.at_z(-2), 3)
    nb_over(p.at_z(2), 4)
    na.arrive(2)
    na.forward(2)
    wg.arrive(4)
    wsend(4)
    rs.step(0)
    over_in(3)
    over_in(4)
    by.step(2)
    gay_slots = [m.slot() for _ in range(2)]
    for i, chain in enumerate((a0, a1s)):
        half_a = chain.last().reshape(2, 128, 128)
        gay_out[i] = half_a.astype(bf16)
        m.send(gay_out.at[i, 1 - yl], gay_in.at[i], gay_slots[i], ylo)
        for h in range(2):
            part[0, h, :, 128 * i : 128 * i + 128] = half_a[h]
    rs.step(1)
    over_in(5)
    over_in(6)
    by.step(3)
    wonward(0, -1, 1)
    over_in(7)
    part[0, 0, :, 256:512] = by.last()
    nb.arrive(3)
    nb.forward(3)
    nb_over(p.at_z(-3), 5)
    nb_over(p.at_z(3), 6)
    na.arrive(3)
    na.forward(3)
    for i in range(2):
        m.wait(gay_in.at[i], gay_slots[i], ylo)
    own_a = part[0, yl, :, 0:256] + jnp.concatenate([gay_in[0], gay_in[1]], axis=1).astype(f32)
    for i in range(2):
        gnorm[:, pl.ds(pl.multiple_of(128 * p.at_x(i), 128), 128)] = own_a[:, 128 * i : 128 * i + 128]
        gnorm[:, pl.ds(pl.multiple_of(128 * p.at_x(2 + i), 128), 128)] = part[0, 0, :, 256 + 128 * i : 384 + 128 * i]
    grad_norm = gnorm[...]
    lat = latent[...].astype(f32)
    inverse = lax.rsqrt(jnp.mean(lat * lat, axis=-1, keepdims=True) + epsilon)
    scaled = grad_norm * gain[...]
    inner = jnp.mean(scaled * lat, axis=-1, keepdims=True)
    pre[:, 0:512] = (inverse * scaled - lat * (inverse * inverse * inverse) * inner).astype(bf16)
    pre_slot = m.slot()
    m.send(pre, pres, pre_slot, sib)
    gsum = jnp.sum(grad_norm * lat * inverse, axis=0, keepdims=True)
    gn[...] = jnp.zeros((8, 128), f32)
    for q in range(4):
        gn[q : q + 1, :] = gsum[:, 128 * q : 128 * q + 128]
    rgz_slots = [m.slot() for _ in range(7)]
    for o in range(1, 8):
        m.send(gn, rgz.at[o - 1], rgz_slots[o - 1], p.dev_z(o))

    nb.arrive(4)
    nb_over(p.at_z(4), 7)
    wonward(-2, 2, -3, 3, 4)
    m.wait(pres, pre_slot, sib)
    both = jnp.concatenate([pre[...], pres[...]], axis=0)

    def gw_tile(i, carry):
        at = pl.ds(4 * i, 4)
        left = jnp.concatenate(
            [intr[c, at].reshape(640, 128), ins[at].reshape(640, 128)], axis=1
        )
        got = nn(left, both[:, 0:512]).astype(bf16)
        for q in range(4):
            piece = got[:, 128 * q : 128 * q + 128].reshape(4, 160, 128)
            gw[q, at] = piece[:, 0:128]
            for j in range(4):
                gw3[4 * (i % 2) + j, q, i // 2] = piece[j, 128:160]
        return carry

    lax.fori_loop(0, 4, gw_tile, 0)
    r3z_slots = [m.slot() for _ in range(7)]
    for o in (4, 3, 5, 2, 6, 1, 7):
        m.send(gw3.at[p.at_z(o)], r3z.at[o - 1], r3z_slots[o - 1], p.dev_z(o))
    r1_slots = [m.slot() for _ in range(3)]
    r2_slots = [m.slot() for _ in range(3)]
    for o in (2, 1, 3):
        m.send(gw.at[p.at_x(o), :, pl.ds(0, 32)], r1.at[o - 1], r1_slots[o - 1], p.dev_x(o))
        hh, ll = p.at_y(o)
        m.send(
            gw.at[:, pl.ds(8 * ll, 8), pl.ds(pl.multiple_of(32 + 48 * hh, 16), 48)],
            r2.at[o - 1], r2_slots[o - 1], p.dev_y(o),
        )

    na.arrive(4)
    for i, o in enumerate((0, -1, 1, -2, 2, -3, 3, 4)):
        nb_arrive(p.at_z(o), i)
    gus_slots = [m.slot() for _ in range(2)]
    for h in range(2):
        lax.fori_loop(2 * h, 2 * h + 2, theirs_tile, 0)
        m.send(gus.at[pl.ds(2 * h, 2)], gusi.at[pl.ds(2 * h, 2)], gus_slots[h], sib)
    gux = [m.slot() for _ in range(6)]
    for h in range(2):
        m.wait(gusi.at[pl.ds(2 * h, 2)], gus_slots[h], sib)
        lax.fori_loop(2 * h, 2 * h + 2, mine_tile, 0)
        for o in (1, 3, 2):
            tiles = pl.ds(2 * h, 2)
            m.send(gu.at[p.at_x(o), tiles], gui.at[o - 1, tiles], gux[3 * h + o - 1], p.dev_x(o))
    rs.step(2)
    rs.step(3)
    turned = rs.last().astype(bf16)
    for o in (1, 7, 2, 6, 3, 5, 4):
        m.wait(r3z.at[o - 1], r3z_slots[o - 1], p.dev_z(o))
    for q in range(4):
        sum3 = gw3[z, q].astype(f32)
        for o in range(7):
            sum3 = sum3 + r3z[o, q].astype(f32)
        a3x[q, 0:64] = sum3.reshape(64, 128).astype(bf16)
        a3x[q, 64:224] = turned
    r3x_slots = [m.slot() for _ in range(3)]
    for o in (2, 1, 3):
        m.send(a3x.at[p.at_x(o)], r3x.at[o - 1], r3x_slots[o - 1], p.dev_x(o))

    for o in range(1, 8):
        m.wait(rgz.at[o - 1], rgz_slots[o - 1], p.dev_z(o))
    gns[0] = gn[...] + jnp.sum(rgz[...], axis=0)
    rgy_slots = [m.slot() for _ in range(3)]
    for o in (1, 2, 3):
        m.send(gns.at[0], rgy.at[o - 1], rgy_slots[o - 1], p.dev_y(o))

    for o in (1, 3, 2):
        m.wait(r1.at[o - 1], r1_slots[o - 1], p.dev_x(o))
    for h in range(2):
        rows = pl.ds(16 * h, 16)
        sum1 = gw[x, :, rows].astype(f32)
        for o in range(3):
            sum1 = sum1 + r1[o, :, rows].astype(f32)
        a1[h] = sum1.astype(bf16)
    ry_slots = [m.slot() for _ in range(3)]
    for o in (2, 1, 3):
        hh, ll = p.at_y(o)
        m.send(a1.at[hh, pl.ds(8 * ll, 8)], ry.at[o - 1], ry_slots[o - 1], p.dev_y(o))
    for o in (1, 3, 2):
        m.wait(r2.at[o - 1], r2_slots[o - 1], p.dev_y(o))
    for q in range(4):
        sum2 = gw[q, pl.ds(8 * yl, 8), pl.ds(pl.multiple_of(32 + 48 * yh, 16), 48)].astype(f32)
        for o in range(3):
            sum2 = sum2 + r2[o, q].astype(f32)
        a2[q] = sum2.astype(bf16)
    rx_slots = [m.slot() for _ in range(3)]
    for o in (2, 1, 3):
        m.send(a2.at[p.at_x(o)], rx.at[o - 1], rx_slots[o - 1], p.dev_x(o))

    for o in (1, 2, 3):
        m.wait(rgy.at[o - 1], rgy_slots[o - 1], p.dev_y(o))
    gns[1] = gns[0] + rgy[0] + rgy[1] + rgy[2]
    rgx_slots = [m.slot() for _ in range(3)]
    for o in (1, 2, 3):
        m.send(gns.at[1], rgx.at[o - 1], rgx_slots[o - 1], p.dev_x(o))

    for o in (1, 3, 2):
        m.wait(r3x.at[o - 1], r3x_slots[o - 1], p.dev_x(o))
    sum3 = a3x[x].astype(f32) + r3x[0].astype(f32) + r3x[1].astype(f32) + r3x[2].astype(f32)
    for ll in range(2):
        for hh in range(2):
            lo = 32 * ll + 16 * hh
            a3y[2 * hh + ll, 0:16] = sum3[lo : lo + 16].astype(bf16)
            a3y[2 * hh + ll, 16:176] = sum3[64:224].astype(bf16)
    r3y_slots = [m.slot() for _ in range(3)]
    for o in (2, 1, 3):
        hh, ll = p.at_y(o)
        m.send(a3y.at[2 * hh + ll], r3y.at[o - 1], r3y_slots[o - 1], p.dev_y(o))

    wlast(0, -1, 1, -2, 2, -3, 3, 4)

    own_columns = pl.multiple_of(2560 * c, 128)

    def gx_tile(i, carry):
        got = nt(both, wc[pl.ds(2 * i, 2)].reshape(640, 640)).astype(bf16)
        gx[:, pl.ds(pl.multiple_of(own_columns + i * 640, 128), 640)] = got[0:128]
        gxs[:, pl.ds(pl.multiple_of(i * 640, 128), 640)] = got[128:256]
        return carry

    lax.fori_loop(0, 4, gx_tile, 0)
    gx_slot = m.slot()
    m.send(gxs, gx.at[:, pl.ds(own_columns, 2560)], gx_slot, sib)
    for o in (1, 3, 2):
        m.wait(ry.at[o - 1], ry_slots[o - 1], p.dev_y(o))
    sum1 = a1[yh, pl.ds(8 * yl, 8)].astype(f32)
    for o in range(3):
        sum1 = sum1 + ry[o].astype(f32)
    a12[:, 0:16] = sum1.astype(bf16)
    for o in (1, 3, 2):
        m.wait(rx.at[o - 1], rx_slots[o - 1], p.dev_x(o))
    sum2 = a2[x].astype(f32)
    for o in range(3):
        sum2 = sum2 + rx[o].astype(f32)
    a12[:, 16:64] = sum2.astype(bf16)
    r12_slots = [m.slot() for _ in range(7)]
    for o in range(1, 8):
        m.send(a12.at[p.at_z(o)], r12.at[o - 1], r12_slots[o - 1], p.dev_z(o))

    for o in (1, 3, 2):
        for h in range(2):
            m.wait(gui.at[o - 1, pl.ds(2 * h, 2)], gux[3 * h + o - 1], p.dev_x(o))
    for h in range(2):
        rows = pl.ds(64 * h, 64)
        total = gu[x, :, rows].astype(f32)
        for o in range(3):
            total = total + gui[o, :, rows].astype(f32)
        guy[h] = total.astype(bf16)
    guy_slot = m.slot()
    m.send(guy.at[1 - yh], guyi, guy_slot, yhi)

    m.wait(guyi, guy_slot, yhi)
    total = guy[yh].astype(f32) + guyi[...].astype(f32)
    for h in range(2):
        guz[h] = total[:, 32 * h : 32 * h + 32].astype(bf16)
    guz_slot = m.slot()
    m.send(guz.at[1 - c], gupb, guz_slot, sib)
    for i in range(4):
        gup[:, pl.ds(pl.multiple_of(1024 * c + 256 * i, 128), 256)] = guz[c, i]

    for o in (1, 2, 3):
        m.wait(rgx.at[o - 1], rgx_slots[o - 1], p.dev_x(o))
    gns[2] = gns[1] + rgx[0] + rgx[1] + rgx[2]
    rgc_slot = m.slot()
    m.send(gns.at[2], rgc, rgc_slot, sib)

    for o in (1, 2, 3):
        m.wait(r3y.at[o - 1], r3y_slots[o - 1], p.dev_y(o))
    sum3 = a3y[2 * yh + yl].astype(f32) + r3y[0].astype(f32) + r3y[1].astype(f32) + r3y[2].astype(f32)
    fin[64:80] = sum3[0:16].astype(bf16)
    rfin[...] = sum3[16:176].astype(bf16)
    rfin_slot = m.slot()
    m.send(rfin, gropeb.at[c], rfin_slot, sib)
    gropeb[c] = rfin[...]
    for o in range(1, 8):
        m.wait(r12.at[o - 1], r12_slots[o - 1], p.dev_z(o))
    fin[0:64] = (a12[z].astype(f32) + jnp.sum(r12[...].astype(f32), axis=0)).astype(bf16)
    fin_slots = [m.slot() for _ in range(3)]
    for slot, friend in zip(fin_slots, (sib, yhi, yhi_other)):
        m.send(fin, glatb.at[c, yh], slot, friend)
    glatb[c, yh] = fin[...]

    m.wait(rgc, rgc_slot, sib)
    total = gns[2] + rgc[...]
    for q in range(4):
        ggain[:, 128 * q : 128 * q + 128] = total[q : q + 1]
    m.wait(gupb, guz_slot, sib)
    for i in range(4):
        gup[:, pl.ds(pl.multiple_of(1024 * (1 - c) + 256 * i, 128), 256)] = gupb[i]

    def columns(first, n, rows):
        row = lax.broadcasted_iota(jnp.int32, (n, 128), 0)
        column = lax.broadcasted_iota(jnp.int32, (n, 128), 1)
        return nt((column == row + first).astype(bf16), rows).astype(bf16)

    m.wait(gropeb.at[1 - c], rfin_slot, sib)
    grope[...] = columns(yl * 64 + p.dp * 4, 16, gropeb[...].reshape(320, 128))[0:4]
    m.wait(glatb.at[1 - c, yh], fin_slots[0], sib)
    m.wait(glatb.at[c, 1 - yh], fin_slots[1], yhi)
    m.wait(glatb.at[1 - c, 1 - yh], fin_slots[2], yhi_other)
    rows = []
    for h in range(2):
        for lo, n in ((0, 16), (16, 48), (64, 16)):
            for i in range(2):
                rows.append(glatb[h, i, lo : lo + n])
    glat[...] = columns((p.dp % 4) * 32, 32, jnp.concatenate(rows, axis=0))
    m.wait(gx.at[:, pl.ds(pl.multiple_of(2560 * (1 - c), 128), 2560)], gx_slot, sib)
    m.finish()


def shards(inputs, latent, gain, w_latent, w_rope, w_up, grad_kv, grad_rope):
    V = lambda *shape: pltpu.VMEM(shape, bf16)
    F = lambda *shape: pltpu.VMEM(shape, f32)
    whole = pl.BlockSpec(memory_space=pltpu.VMEM)
    scratch = dict(
        inputs=V(128, 5120), kv=V(2, 8, 128, 2048), up=V(16, 32, 2048), nrm=V(2, 8, 512, 128), part=F(8, 2, 128, 512),
        ga_out=V(2, 8, 256, 128), ga_p=V(2, 4, 256, 128), ga_m=V(2, 4, 256, 128),
        gy_out=V(8, 128, 256), gy_in=V(8, 128, 256),
        gb_out=V(8, 128, 256), gb_p=V(4, 128, 256), gb_m=V(4, 128, 256),
        gay_out=V(2, 2, 128, 128), gay_in=V(2, 128, 128), gnorm=F(128, 512),
        wx=V(320, 640), wq=V(8, 80, 640), wa=V(80, 640), wc=V(8, 320, 640), intr=V(2, 16, 160, 128), ins=V(16, 160, 128),
        pre=V(128, 640), pres=V(128, 640), gxs=V(128, 2560),
        rp=V(128, 128), rps=V(128, 128), gw=V(4, 16, 128, 128), gw3=V(8, 4, 2, 32, 128), r1=V(3, 16, 32, 128), r2=V(3, 4, 8, 48, 128), r3z=V(7, 4, 2, 32, 128),
        a1=V(2, 16, 16, 128), a2=V(4, 8, 48, 128),
        s3=V(8, 160, 128), s3p=V(4, 160, 128), s3m=V(4, 160, 128),
        a3x=V(4, 224, 128), r3x=V(3, 224, 128), ry=V(3, 8, 16, 128), rx=V(3, 8, 48, 128),
        a12=V(8, 64, 128), r12=V(7, 64, 128), a3y=V(4, 176, 128), r3y=V(3, 176, 128),
        fin=V(80, 128), rfin=V(160, 128), glatb=V(2, 2, 80, 128), gropeb=V(2, 160, 128), gupb=V(4, 32, 256),
        gus=V(4, 512, 256), gusi=V(4, 512, 256), gu=V(4, 4, 128, 256), gui=V(3, 4, 128, 256),
        guy=V(2, 4, 64, 256), guyi=V(4, 64, 256), guz=V(2, 4, 32, 256),
        gn=F(8, 128), rgz=F(7, 8, 128), rgy=F(3, 8, 128), rgx=F(3, 8, 128), rgc=F(8, 128), gns=F(3, 8, 128),
        kv_sem=pltpu.SemaphoreType.DMA((2,)),
        send_sem=pltpu.SemaphoreType.DMA((SENDS + 1,)),
        recv_sem=pltpu.SemaphoreType.DMA((RECVS,)),
    )

    def body(*refs):
        own = refs[:13]
        kernel(*own, **dict(zip(scratch, refs[13:])))

    gx, gup, glat, grope, ggain = pl.pallas_call(
        body,
        out_shape=(
            jax.ShapeDtypeStruct((128, 5120), bf16),
            jax.ShapeDtypeStruct((32, 2048), bf16),
            jax.ShapeDtypeStruct((32, 320), bf16),
            jax.ShapeDtypeStruct((4, 320), bf16),
            jax.ShapeDtypeStruct((1, 512), f32),
        ),
        in_specs=[pl.BlockSpec(memory_space=pl.ANY)] + [whole] * 5 + [pl.BlockSpec(memory_space=pl.ANY), whole],
        out_specs=(whole,) * 5,
        scratch_shapes=list(scratch.values()),
        compiler_params=pltpu.CompilerParams(
            collective_id=0, has_side_effects=True, vmem_limit_bytes=60 << 20
        ),
    )(
        inputs, latent, gain.reshape(1, 512), w_latent, w_rope.T, w_up,
        grad_kv.reshape(2, 8, 128, 2048), grad_rope.T,
    )

    def hand_over(*refs):
        for i in range(5):
            refs[5 + i][...] = refs[i][...]

    made = (gx, gup, glat, grope, ggain)
    gx, gup, glat, grope, ggain = pl.pallas_call(
        hand_over,
        out_shape=tuple(jax.ShapeDtypeStruct(a.shape, a.dtype) for a in made),
        in_specs=[whole] * 5,
        out_specs=(whole,) * 5,
    )(*made)
    return gx, gup, glat.T, grope.T, ggain.reshape(512)


def solution(mesh):
    in_specs = (
        P(("dp", "tensor"), None),
        P(("dp", "tensor"), None),
        P(),
        P("tensor", None),
        P("tensor", None),
        P("dp", "tensor"),
        P("dp", "tensor"),
        P(("dp", "tensor"), None),
    )
    out_specs = (
        P(("dp", "tensor"), None),
        P("dp", "tensor"),
        P("tensor", "dp"),
        P("tensor", "dp"),
        P(),
    )
    return jax.shard_map(shards, mesh=mesh, in_specs=in_specs, out_specs=out_specs, check_vma=False)
```
